128 devices in a mesh: rows: 32 (over z, x, core), branch: 4 (over y).
Axes of the slice: x: 4, y: 4, z: 4, core: 2. Of those that a mesh axis runs over, the one named last changes fastest.
Arguments:
- logits: bfloat16 [19, 256, 1024], P(None, 'rows'), may hold values from -20 to 360, as said below
- labels: int32 [256, 1024], P('rows'), may hold values from 0 to 18
- pixel_weight: float32 [256, 1024], P('rows'), may hold values from 0.05 to 3.1, as said below
- head_weight: bfloat16 [32, 19], replicated, may hold values from -1.25 to 1.25
- deriv_inner: bfloat16 [4, 32, 8, 32, 1024], P('branch', 'rows'), may hold values from 0.05 to 1, as said below
- deriv_outer: bfloat16 [4, 32, 8, 32, 1024], P('branch', 'rows'), may hold values from 0.05 to 0.7, as said below
- conv_inner: bfloat16 [4, 9, 256, 256], P('branch'), may hold values from -6 to 6
- conv_outer: bfloat16 [4, 9, 256, 256], P('branch'), may hold values from -6 to 6
- join_weight: bfloat16 [4, 4, 256, 256], replicated, may hold values from -6 to 6
Outputs:
- adjoint: float32 [4, 32, 8, 32, 1024], P('branch', 'rows')
The draws below stay inside these ranges and needn't reach their ends.
Inputs may be any that keep to these rules, and one draw needn't show every extreme that they name: `logits`: saved class scores of the forward pass. `pixel_weight`: positive loss weights. `deriv_inner`: saved derivatives of the inner activation. `deriv_outer`: saved derivatives of the outer activation.
All inputs are finite; a program needn't handle non-finite values.
Results may differ from the reference program's by a relative error of at most 0.022.
Values may be sent and summed in bfloat16 or wider, within the bound.
A program may use at most 192 MiB of HBM per device.

```python
import jax
import jax.numpy as jnp
from jax import lax

BASE_CH = 32
CLASSES = 19
BRANCHES = 4
ROWS_DEV = 8
WIDTH = 1024
ITERS = 3
PIECES = 32
TOTAL_ROWS = 256


def draw_logits(key, part):
    key = jax.random.fold_in(key, 17)
    subkeys = jax.random.split(key, 1)
    full_shape = (CLASSES, TOTAL_ROWS, WIDTH)
    scores = jnp.clip(3.0 * jax.random.normal(subkeys[0], full_shape, jnp.float32), -18.0, 18.0)
    return scores.astype(jnp.bfloat16)


def draw_pixel_weight(key, part):
    key = jax.random.fold_in(key, 29)
    spread = jax.random.uniform(key, (TOTAL_ROWS, WIDTH), jnp.float32)
    position = jnp.arange(TOTAL_ROWS, dtype=jnp.float32) / (TOTAL_ROWS - 1)
    ramp = 0.4 + position
    rough = 0.5 + spread
    return (ramp[:, None] * rough).astype(jnp.float32)


def slab_profile(key, lower, upper, steepness):
    fresh = jax.random.uniform(key, (BRANCHES, PIECES, ROWS_DEV, BASE_CH, WIDTH), jnp.float32)
    position = jnp.arange(PIECES, dtype=jnp.float32) / (PIECES - 1)
    exponent = jnp.exp(steepness * (2.0 * position - 1.0))[None, :, None, None, None]
    return lower + (upper - lower) * jnp.power(fresh, exponent)


def draw_deriv_inner(key, part):
    key = jax.random.fold_in(key, 41)
    values = slab_profile(key, 0.05, 1.0, 2.5)
    return values.astype(jnp.bfloat16)


def draw_deriv_outer(key, part):
    key = jax.random.fold_in(key, 53)
    values = slab_profile(key, 0.05, 0.7, 2.5)
    return values.astype(jnp.bfloat16)


def set_ends(entries, rng, low, top_value):
    longest = entries.shape.index(max(entries.shape))
    spots = []
    for shift in (0, 1):
        where = [jax.random.randint(jax.random.fold_in(rng, axis), (), 0, length) for axis, length in enumerate(entries.shape)]
        where[longest] = (where[longest] + shift) % entries.shape[longest]
        spots.append(tuple(where))
    return entries.at[spots[0]].set(low).at[spots[1]].set(top_value)


def block_scale(own_key, shape, shards, low, high):
    def one(dim, shards_of):
        heights = jax.random.uniform(jax.random.fold_in(jax.random.fold_in(own_key, 6), dim), (shards_of,), jnp.float32, low / len(shards), high / len(shards))
        return jnp.repeat(jnp.exp(heights), shape[dim] // shards_of).reshape((-1,) + (1,) * (len(shape) - dim - 1))

    gain = one(*shards[0])
    for cut in shards[1:]:
        gain = gain * one(*cut)
    return gain


def centred(rng, extent, scale, most, cuts=(), kind=jnp.bfloat16):
    entries = jax.random.normal(rng, extent, jnp.float32) * scale
    if len(cuts) > 0:
        entries = block_scale(rng, extent, cuts, -0.22, 0.18) * entries
    return jnp.clip(entries, min=-most, max=most).astype(kind)


def setup_inputs(seed: int = 0) -> dict:
    key_list = jax.random.split(jax.random.key(seed), 10)
    logits = draw_logits(jax.random.fold_in(key_list[9], 71), 0)
    labels = set_ends(jax.random.randint(key_list[1], (TOTAL_ROWS, WIDTH), 0, CLASSES), jax.random.fold_in(key_list[1], 1), 0, CLASSES - 1).astype(jnp.int32)
    pixel_weight = draw_pixel_weight(jax.random.fold_in(key_list[9], 71), 0)
    head_weight = centred(key_list[3], (BASE_CH, CLASSES), CLASSES ** -0.5, 1.25)
    deriv_inner = draw_deriv_inner(jax.random.fold_in(key_list[9], 71), 0)
    deriv_outer = draw_deriv_outer(jax.random.fold_in(key_list[9], 71), 0)
    conv_inner = centred(key_list[6], (BRANCHES, 9, 8 * BASE_CH, 8 * BASE_CH), 1.0, 6.0, ((0, 4),))
    conv_outer = centred(key_list[7], (BRANCHES, 9, 8 * BASE_CH, 8 * BASE_CH), 1.0, 6.0, ((0, 4),))
    join_weight = centred(key_list[8], (BRANCHES, BRANCHES, 8 * BASE_CH, 8 * BASE_CH), 1.0, 6.0)
    return {"logits": logits, "labels": labels, "pixel_weight": pixel_weight, "head_weight": head_weight, "deriv_inner": deriv_inner, "deriv_outer": deriv_outer, "conv_inner": conv_inner, "conv_outer": conv_outer, "join_weight": join_weight}


def unpack_map(packed, branch_level):
    row_count = ROWS_DEV >> branch_level
    channels = BASE_CH << branch_level
    columns = WIDTH >> branch_level
    return packed[branch_level, :, :row_count].reshape(PIECES * row_count, channels, columns)


def pack_maps(grids):
    blocks = []
    for branch_level in range(BRANCHES):
        row_count = ROWS_DEV >> branch_level
        shaped = grids[branch_level].reshape(PIECES, row_count, BASE_CH, WIDTH)
        blocks.append(jnp.pad(shaped, ((0, 0), (0, ROWS_DEV - row_count), (0, 0), (0, 0))))
    return jnp.stack(blocks)


def conv_transpose(kernels, grid_map):
    height, channels, columns = grid_map.shape
    padded = jnp.pad(grid_map.astype(jnp.float32), ((1, 1), (0, 0), (1, 1)))
    weights_wide = kernels.astype(jnp.float32)
    summed = jnp.zeros((height, channels, columns), jnp.float32)
    for kernel_tap in range(9):
        row_shift = kernel_tap // 3 - 1
        col_shift = kernel_tap % 3 - 1
        window = padded[1 - row_shift:1 - row_shift + height, :, 1 - col_shift:1 - col_shift + columns]
        summed = summed + jnp.einsum("oi,roq->riq", weights_wide[kernel_tap], window)
    return summed * (9 * channels) ** -0.5


def pool_sum(grid_map, factor):
    height, channels, columns = grid_map.shape
    return grid_map.reshape(height // factor, factor, channels, columns // factor, factor).sum(axis=(1, 4))


def contribution(join_weight, source, level_from, level_to):
    mixing = join_weight[level_from, level_to, :BASE_CH << level_from, :BASE_CH << level_to].astype(jnp.float32)
    factor_scale = (BASE_CH << level_to) ** -0.5
    if level_to < level_from:
        factor = 2 ** (level_from - level_to)
        mixed = jnp.einsum("oi,roq->riq", mixing, source.astype(jnp.float32))
        mixed = (mixed * (factor_scale / (factor * factor))).astype(jnp.bfloat16)
        return jnp.repeat(jnp.repeat(mixed, factor, axis=0), factor, axis=2)
    factor = 2 ** (level_to - level_from)
    pooled = pool_sum(source.astype(jnp.float32), factor)
    mixed = jnp.einsum("oi,roq->riq", mixing, pooled, precision=lax.Precision.HIGHEST)
    return (mixed * factor_scale).astype(jnp.bfloat16)


def adjoint_map(field, deriv_inner, deriv_outer, conv_inner, conv_outer, join_weight):
    scaled_map = (deriv_outer.astype(jnp.float32) * field).astype(jnp.bfloat16)
    scaled_grids = [unpack_map(scaled_map, position) for position in range(BRANCHES)]
    inner_grids = []
    for position in range(BRANCHES):
        channels = BASE_CH << position
        inner_grids.append(conv_transpose(conv_outer[position, :, :channels, :channels], scaled_grids[position]))
    inner_map = pack_maps(inner_grids)
    w_map = (deriv_inner.astype(jnp.float32) * inner_map).astype(jnp.bfloat16)
    conv_grids = []
    for position in range(BRANCHES):
        channels = BASE_CH << position
        conv_grids.append(conv_transpose(conv_inner[position, :, :channels, :channels], unpack_map(w_map, position)))
    conv_part = pack_maps(conv_grids)
    joined_grids = []
    for receiver in range(BRANCHES):
        summed = jnp.zeros(scaled_grids[receiver].shape, jnp.float32)
        for sender in range(BRANCHES):
            if sender != receiver:
                summed = summed + contribution(join_weight, scaled_grids[sender], sender, receiver).astype(jnp.float32)
        joined_grids.append(summed)
    joined = pack_maps(joined_grids)
    return scaled_map.astype(jnp.float32) + conv_part + joined


def inner_product(first_vec, second_vec):
    return jnp.sum(first_vec * second_vec)


def reference(logits, labels, pixel_weight, head_weight, deriv_inner, deriv_outer, conv_inner, conv_outer, join_weight):
    probabilities = jax.nn.softmax(logits.astype(jnp.float32), axis=0)
    classes = jnp.arange(CLASSES, dtype=jnp.int32)[:, None, None]
    onehot = (labels[None] == classes).astype(jnp.float32)
    err = (pixel_weight[None] * (probabilities - onehot)).astype(jnp.bfloat16)
    first_map = jnp.einsum("ck,khq->hcq", head_weight.astype(jnp.float32), err.astype(jnp.float32))
    grids = [first_map]
    for position in range(1, BRANCHES):
        grids.append(jnp.zeros((TOTAL_ROWS >> position, BASE_CH << position, WIDTH >> position), jnp.float32))
    loss_source = pack_maps(grids)
    iterate = jnp.zeros_like(loss_source)
    previous = loss_source
    update = loss_source
    lefts = []
    rights = []
    for iteration in range(ITERS):
        iterate = iterate + update
        current = adjoint_map(iterate, deriv_inner, deriv_outer, conv_inner, conv_outer, join_weight) + loss_source - iterate
        change = current - previous
        previous = current
        along_right = [inner_product(right_vec, change) for right_vec in rights]
        along_left = [inner_product(update, left_vec) for left_vec in lefts]
        right_new = -update
        for slot_index in range(len(rights)):
            right_new = right_new + along_left[slot_index] * rights[slot_index]
        curvature = inner_product(right_new, change)
        left_new = update + change
        for slot_index in range(len(lefts)):
            left_new = left_new - along_right[slot_index] * lefts[slot_index]
        left_new = left_new / curvature
        lefts.append(left_new)
        rights.append(right_new)
        update = current
        for slot_index in range(len(lefts)):
            update = update - inner_product(rights[slot_index], current) * lefts[slot_index]
    return iterate + update
```

```python
from functools import partial

import jax
import jax.numpy as jnp
from jax import lax
from jax.experimental import pallas as pl
from jax.experimental.pallas import tpu as pltpu
from jax.sharding import PartitionSpec as P

BASE_CH = 32
BRANCHES = 4
ITERS = 3
GROUP = (6, 2, 1, 1)
MESH = pl.DeviceIdType.MESH
BF16 = jnp.bfloat16
F32 = jnp.float32


def dot(left, right):
    return jnp.dot(left, right, preferred_element_type=F32)


def dot_nt(left, right):
    return lax.dot_general(left, right, (((1,), (1,)), ((), ())), preferred_element_type=F32)


def iotas(shape):
    return lax.broadcasted_iota(jnp.int32, shape, 0), lax.broadcasted_iota(jnp.int32, shape, 1)


def flags(mask):
    return jnp.where(mask, 1.0, 0.0).astype(BF16)


def shift_cols(values, by):
    width = values.shape[1]
    _, col = iotas(values.shape)
    if by == 1:
        return jnp.where(col == 0, 0.0, pltpu.roll(values, 1, 1))
    return jnp.where(col == width - 1, 0.0, pltpu.roll(values, width - 1, 1))


def wait_all(ref, sem):
    pltpu.make_async_copy(ref, ref, sem).wait()


def kernel(
    pieces,
    across,
    logits,
    labels,
    pixel_weight,
    head_weight,
    deriv_inner,
    deriv_outer,
    conv_inner,
    conv_outer,
    join_weight,
    out,
    s_logits,
    s_labels,
    s_pixel,
    s_head,
    outer,
    inner,
    k_outer,
    k_inner,
    k_join,
    band0,
    band1,
    band2,
    band3,
    mix,
    pool2,
    pool4,
    pool8,
    up2,
    up4,
    up8,
    scaled,
    wmap,
    vecs,
    give01,
    give02,
    give03,
    give12,
    give13,
    give23,
    take01,
    take02,
    take03,
    take12,
    take13,
    take23,
    part,
    took_pair,
    part_pair,
    took,
    in_sem,
    rim_send,
    rim_recv,
    halo_send,
    halo_recv,
    join_send,
    join_recv,
    sum_send,
    sum_recv,
):
    piece = lax.axis_index("rows")
    branch = lax.axis_index("branch")
    full_rows, width = outer.shape[0], outer.shape[2]
    row_count = jnp.right_shift(jnp.int32(full_rows), branch)
    bands = (band0, band1, band2, band3)
    gives = {(0, 1): give01, (0, 2): give02, (0, 3): give03, (1, 2): give12, (1, 3): give13, (2, 3): give23}
    takes = {(0, 1): take01, (0, 2): take02, (0, 3): take03, (1, 2): take12, (1, 3): take13, (2, 3): take23}
    has_above = piece > 0
    has_below = piece < pieces - 1
    core, chip_x, chip_z = lax.rem(piece, 2), lax.rem(piece // 2, across), piece // (2 * across)
    deep = pieces // (2 * across)

    def sizes(level):
        return full_rows >> level, BASE_CH << level, width >> level, 1 << level

    def hops(offset):
        return sum(min(step, size - step) for step, size in zip(offset, (across, deep, BRANCHES)))

    offsets = [
        (x, z, y) for x in range(across) for z in range(deep) for y in range(BRANCHES) if x or z or y
    ]
    offsets.sort(key=hops, reverse=True)
    partner = (piece + 1 - 2 * core, branch)

    def chip_peer(offset):
        x = lax.rem(chip_x + offset[0], across)
        z = lax.rem(chip_z + offset[1], deep)
        return ((z * across + x) * 2 + core, lax.rem(branch + offset[2], BRANCHES))

    near = [(lax.rem(piece + step, pieces), branch) for step in (1, 2, pieces - 2, pieces - 1)]
    greeted = [chip_peer(offset) for offset in offsets] + near + [partner]

    def on(level):
        return pl.when(branch == level)

    def input_copies(level):
        rows, chans, _, _ = sizes(level)
        lanes = max(chans, 128)
        pairs = []
        if level == 0:
            pairs += [(logits, s_logits), (labels, s_labels), (pixel_weight, s_pixel), (head_weight, s_head)]
        pairs += [
            (deriv_outer.at[0, 0, pl.ds(0, rows)], outer.at[pl.ds(0, rows)]),
            (conv_outer.at[0, :, pl.ds(0, chans), pl.ds(0, lanes)], k_outer.at[:, pl.ds(0, chans), pl.ds(0, lanes)]),
            (conv_inner.at[0, :, pl.ds(0, chans), pl.ds(0, lanes)], k_inner.at[:, pl.ds(0, chans), pl.ds(0, lanes)]),
            (deriv_inner.at[0, 0, pl.ds(0, rows)], inner.at[pl.ds(1, rows)]),
        ]
        for other in range(level):
            few = BASE_CH << other
            pairs.append((join_weight.at[level, other, pl.ds(0, chans)], k_join.at[other, pl.ds(0, chans)]))
            pairs.append((join_weight.at[other, level, pl.ds(0, few)], k_join.at[3 + other, pl.ds(0, few)]))
        return [pltpu.make_async_copy(src, dst, in_sem.at[at]) for at, (src, dst) in enumerate(pairs)]

    for level in range(BRANCHES):

        @on(level)
        def _(level=level):
            for copy in input_copies(level):
                copy.start()

    barrier = pltpu.get_barrier_semaphore()
    for peer in greeted:
        pl.semaphore_signal(barrier, inc=1, device_id=peer, device_id_type=MESH)

    for ref, factor in ((pool2, 2), (pool4, 4), (pool8, 8)):
        row, col = iotas(ref.shape)
        ref[...] = flags(row // factor == col)
    for ref, factor in ((up2, 2), (up4, 4), (up8, 8)):
        row, col = iotas(ref.shape)
        ref[...] = flags(row == col // factor)

    @pl.when(jnp.logical_not(has_above))
    def _():
        inner[0] = jnp.zeros(inner.shape[1:], BF16)
        for turn in range(ITERS):
            for slot in (0, 1):
                scaled[turn, slot] = jnp.zeros(inner.shape[1:], BF16)

    for level in range(BRANCHES):
        rows = sizes(level)[0]

        @pl.when(jnp.logical_and(branch == level, jnp.logical_not(has_below)))
        def _(rows=rows):
            inner[rows + 1] = jnp.zeros(inner.shape[1:], BF16)
            for turn in range(ITERS):
                for slot in (rows + 2, rows + 3):
                    scaled[turn, slot] = jnp.zeros(inner.shape[1:], BF16)

    @pl.when(jnp.logical_and(branch == 3, piece == 1))
    def _():
        for turn in range(ITERS):
            scaled[turn, 0] = jnp.zeros(inner.shape[1:], BF16)

    @pl.when(jnp.logical_and(branch == 3, piece == pieces - 2))
    def _():
        for turn in range(ITERS):
            scaled[turn, 4] = jnp.zeros(inner.shape[1:], BF16)

    def shuffle(level):
        chans, factor = BASE_CH << level, 1 << level
        row, col = iotas((chans, chans))
        return flags(col == factor * lax.rem(row, BASE_CH) + row // BASE_CH)

    def prepare(level):
        rows, chans, _, _ = sizes(level)
        many = GROUP[level]
        order = shuffle(level)
        for which, kernels in enumerate((k_outer, k_inner)):
            for dx in range(3):
                taps = [kernels[3 * dy + dx, :chans, :chans] for dy in (2, 1, 0)]
                if level > 0:
                    taps = [dot(order, tap).astype(BF16) for tap in taps]
                line = dot_nt(order, jnp.concatenate(taps, axis=0)).astype(BF16)
                if many == 1:
                    bands[level][which, dx * chans : (dx + 1) * chans, :] = line
                else:
                    for row_out in range(many):
                        at, to = iotas((3 * chans, (many + 2) * chans))
                        placed = dot(line, flags(to == at + row_out * chans))
                        start = (dx * many + row_out) * chans
                        bands[level][which, start : start + chans, :] = placed.astype(BF16)
        for other in range(level):
            few = BASE_CH << other
            sent = dot(order, k_join[other, :chans, :few]).astype(BF16)
            mix[other, :few, :chans] = dot_nt(shuffle(other), sent).astype(BF16)
            got = dot(shuffle(other), k_join[3 + other, :few, :chans]).astype(BF16)
            mix[3 + other, :chans, :few] = dot_nt(order, got).astype(BF16)

    @on(0)
    def _():
        for copy in input_copies(0)[:5]:
            copy.wait()
        scores = s_logits[...].astype(F32)
        powers = jnp.exp(scores - jnp.max(scores, axis=0, keepdims=True))
        shares = powers / jnp.sum(powers, axis=0, keepdims=True)
        classes = lax.broadcasted_iota(jnp.int32, scores.shape, 0)
        hits = jnp.where(s_labels[...][None] == classes, 1.0, 0.0)
        err = s_pixel[...][None] * (shares - hits)
        count = scores.shape[0]
        flat = err.reshape(count * full_rows, width).astype(BF16)
        row, col = iotas((full_rows * BASE_CH, BASE_CH))
        tall = dot_nt(flags(lax.rem(row, BASE_CH) == col), s_head[...]).astype(BF16)
        row, col = iotas((count, count * full_rows))
        wide = dot(tall, flags(row == col // full_rows))
        row, col = iotas(wide.shape)
        head = jnp.where(row // BASE_CH == lax.rem(col, full_rows), wide, 0.0).astype(BF16)
        first = dot(head, flat)
        for row in range(full_rows):
            own = first[row * BASE_CH : (row + 1) * BASE_CH]
            vecs[0, row] = own
            scaled[0, 2 + row] = (outer[row].astype(F32) * own).astype(BF16)

    @pl.when(branch > 0)
    def _():
        def clear(row, _):
            vecs[0, row] = jnp.zeros(vecs.shape[2:], F32)
            return 0

        lax.fori_loop(0, row_count, clear, 0)

    pl.semaphore_wait(barrier, len(greeted))

    def rim_copy(level, below):
        rows = sizes(level)[0]
        if below:
            return pltpu.make_async_remote_copy(
                deriv_inner.at[0, 0, rows - 1], inner.at[0], rim_send.at[0], rim_recv.at[0],
                device_id=(piece + 1, branch), device_id_type=MESH,
            )
        return pltpu.make_async_remote_copy(
            deriv_inner.at[0, 0, 0], inner.at[rows + 1], rim_send.at[1], rim_recv.at[1],
            device_id=(piece - 1, branch), device_id_type=MESH,
        )

    def send_rim(level):
        @pl.when(has_below)
        def _():
            rim_copy(level, True).start()

        @pl.when(has_above)
        def _():
            rim_copy(level, False).start()

    def wait_rim(level):
        rows = sizes(level)[0]

        @pl.when(has_above)
        def _():
            wait_all(inner.at[0], rim_recv.at[0])

        @pl.when(has_below)
        def _():
            wait_all(inner.at[rows + 1], rim_recv.at[1])

    def halo_copies(level, turn):
        rows = sizes(level)[0]
        if level < 3:
            plan = [
                (1, slice(rows, rows + 2), slice(0, 2)),
                (-1, slice(2, 4), slice(rows + 2, rows + 4)),
            ]
        else:
            plan = [
                (1, slice(2, 3), slice(1, 2)),
                (-1, slice(2, 3), slice(3, 4)),
                (2, slice(2, 3), slice(0, 1)),
                (-2, slice(2, 3), slice(4, 5)),
            ]
        result = []
        for at, (step, src, dst) in enumerate(plan):
            there = piece + step
            source = piece - step
            copy = pltpu.make_async_remote_copy(
                scaled.at[turn, pl.ds(src.start, src.stop - src.start)],
                scaled.at[turn, pl.ds(dst.start, dst.stop - dst.start)],
                halo_send.at[turn, at],
                halo_recv.at[turn, at],
                device_id=(there, branch),
                device_id_type=MESH,
            )
            sends = there < pieces if step > 0 else there >= 0
            gets = source >= 0 if step > 0 else source < pieces
            result.append((sends, copy, gets))
        return result

    def send_halo(level, turn):
        for sends, copy, _ in halo_copies(level, turn):

            @pl.when(sends)
            def _(copy=copy):
                copy.start()

    def join_copy(level, other, turn):
        pair = (min(level, other), max(level, other))
        return pltpu.make_async_remote_copy(
            gives[pair].at[turn], takes[pair].at[turn], join_send.at[turn, other], join_recv.at[turn, level],
            device_id=(piece, jnp.int32(other)), device_id_type=MESH,
        )

    def chunks(block, level):
        span = width >> level
        return [block[:, at * span : (at + 1) * span] for at in range(1 << level)]

    def grid_rows(load, slots, level):
        return jnp.concatenate([part for slot in slots for part in chunks(load(slot), level)], axis=0)

    def send_terms(level, turn):
        rows, chans, cols, _ = sizes(level)
        load = lambda slot: scaled[turn, slot]
        own = grid_rows(load, range(2, 2 + rows), level)
        for other in range(level + 1, BRANCHES):
            factor = 1 << (other - level)
            height, less = rows // factor, cols // factor
            ref = gives[(level, other)]
            if factor == 2:
                spans = [(at, pool2[...]) for at in range(cols // 256)]
                pieces_of = [dot(own[:, at * 256 : (at + 1) * 256], mat) for at, mat in spans]
            else:
                mat = pool4[:cols, :less] if factor == 4 else pool8[:cols, :less]
                pieces_of = [dot(own, mat)]
            for at, part in enumerate(pieces_of):
                span = part.shape[1]
                for row in range(height):
                    summed = part[row * factor * chans : (row * factor + 1) * chans]
                    for extra in range(1, factor):
                        start = (row * factor + extra) * chans
                        summed = summed + part[start : start + chans]
                    ref[turn, row * chans : (row + 1) * chans, at * span : (at + 1) * span] = summed.astype(BF16)
            join_copy(level, other, turn).start()
        for other in range(level):
            few = BASE_CH << other
            factor = 1 << (level - other)
            scale = few ** (-0.5) / (factor * factor)
            ref = gives[(other, level)]
            matrix = mix[other, :few, :chans]
            for row in range(rows):
                mixed = dot(matrix, own[row * chans : (row + 1) * chans])
                ref[turn, row * few : (row + 1) * few, :] = (mixed * scale).astype(BF16)
            join_copy(level, other, turn).start()

    def conv(level, which, load, first, many):
        _, chans, _, _ = sizes(level)
        most = GROUP[level]
        band = bands[level]
        right = grid_rows(load, range(first, first + many + 2), level)
        if many == most:
            left = band[which]
        else:
            left = jnp.concatenate(
                [
                    band[which, dx * most * chans : (dx * most + many) * chans, : (many + 2) * chans]
                    for dx in range(3)
                ],
                axis=0,
            )
        prod = dot(left, right)
        size = many * chans
        return prod[size : 2 * size] + shift_cols(prod[2 * size :], 1) + shift_cols(prod[:size], -1)

    def conv_lanes(level, which, load, first, many):
        _, chans, cols, _ = sizes(level)
        right = jnp.concatenate(
            [grid_rows(load, range(first + at, first + at + 3), level) for at in range(many)], axis=1
        )
        prod = dot(bands[level][which], right)
        result = []
        for at in range(many):
            own = prod[:, at * cols : (at + 1) * cols]
            result.append(
                own[chans : 2 * chans] + shift_cols(own[2 * chans :], 1) + shift_cols(own[:chans], -1)
            )
        return result

    def put_w(level, row, values):
        _, chans, cols, factor = sizes(level)
        scale = (9 * chans) ** (-0.5)
        for at in range(factor):
            lanes = slice(at * cols, (at + 1) * cols)
            part = values[at * BASE_CH : (at + 1) * BASE_CH] * scale
            wmap[row + 1, :, lanes] = (inner[row + 1, :, lanes].astype(F32) * part).astype(BF16)

    def put_out(level, turn, to, row, values):
        _, chans, cols, factor = sizes(level)
        scale = (9 * chans) ** (-0.5)
        for at in range(factor):
            lanes = slice(at * cols, (at + 1) * cols)
            part = values[at * BASE_CH : (at + 1) * BASE_CH] * scale
            vecs[to, row, :, lanes] = scaled[turn, 2 + row, :, lanes].astype(F32) + part

    def outer_conv(level, turn, starts):
        chans = BASE_CH << level
        load = lambda slot: scaled[turn, slot]
        for first, many in starts:
            if level == 3:
                for at, values in enumerate(conv_lanes(level, 0, load, first + 1, many)):
                    put_w(level, first + at, values)
            else:
                values = conv(level, 0, load, first + 1, many)
                for at in range(many):
                    put_w(level, first + at, values[at * chans : (at + 1) * chans])

    def inner_conv(level, turn, to, starts):
        chans = BASE_CH << level
        load = lambda slot: wmap[slot]
        for first, many in starts:
            if level == 3:
                for at, values in enumerate(conv_lanes(level, 1, load, first, many)):
                    put_out(level, turn, to, first + at, values)
            else:
                values = conv(level, 1, load, first, many)
                for at in range(many):
                    put_out(level, turn, to, first + at, values[at * chans : (at + 1) * chans])

    inside = ([(1, 6)], [(1, 2)], [], [])
    edges = ([(-1, 2), (7, 2)], [(-1, 2), (3, 2)], [(-1, 1), (0, 1), (1, 1), (2, 1)], [(-1, 3)])
    early = ([(2, 4)], [], [], [])
    finals = ([(0, 2), (6, 2)], [(0, 2), (2, 2)], [(0, 1), (1, 1)], [(0, 1)])
    order = ((0, 1, 6, 7, 2, 3, 4, 5), (0, 1, 2, 3), (0, 1), (0,))
    rims = (4, 4, 2, 1)

    def convs_before(level, turn, to):
        outer_conv(level, turn, inside[level])
        inner_conv(level, turn, to, early[level])

    def convs_after(level, turn, to):
        for _, copy, gets in halo_copies(level, turn):

            @pl.when(gets)
            def _(copy=copy):
                copy.wait_recv()

        outer_conv(level, turn, edges[level])
        inner_conv(level, turn, to, finals[level])

    def term_rows(level, other, turn):
        rows, chans, cols, _ = sizes(level)
        pair = (min(level, other), max(level, other))
        ref = takes[pair]
        wait_all(ref.at[turn], join_recv.at[turn, other])
        if other < level:
            less = BASE_CH << other
            matrix = mix[3 + other, :chans, :less]
            scale = chans ** (-0.5)
            mixed = [dot(matrix, ref[turn, row * less : (row + 1) * less, :]) for row in range(rows)]
            return [(value * scale).astype(BF16).astype(F32) for value in mixed]
        times = 1 << (other - level)
        got = ref[turn]
        if times == 2:
            wide = jnp.concatenate(
                [dot(got[:, at * 128 : (at + 1) * 128], up2[...]) for at in range(cols // 256)], axis=1
            )
        else:
            wide = dot(got, up4[: cols // 4, :cols] if times == 4 else up8[: cols // 8, :cols])
        starts = [(row // times) * chans for row in range(rows)]
        return [wide[start : start + chans] for start in starts]

    def finish(level, turn):
        _, _, cols, factor = sizes(level)
        to = turn + 1
        others = [other for other in range(BRANCHES) if other != level and (turn > 0 or other == 0)]
        terms = [term_rows(level, other, turn) for other in others]
        for done, row in enumerate(order[level]):
            for at in range(factor):
                lanes = slice(at * cols, (at + 1) * cols)
                parts = [] if level > 0 and turn == 0 else [vecs[to, row, :, lanes]]
                parts += [term[row][at * BASE_CH : (at + 1) * BASE_CH] for term in terms]
                value = parts[0]
                for more in parts[1:]:
                    value = value + more
                vecs[to, row, :, lanes] = value
                if to < ITERS:
                    scaled[to, 2 + row, :, lanes] = (outer[row, :, lanes].astype(F32) * value).astype(BF16)
            if to < ITERS and done + 1 == rims[level]:
                send_halo(level, to)

    def products(pairs):
        def step(row, sums):
            result = []
            for have, (left, right) in zip(sums, pairs):
                prod = vecs[left, row] * vecs[right, row]
                result.append(have + ((prod[0:8] + prod[8:16]) + (prod[16:24] + prod[24:32])))
            return tuple(result)

        zero = jnp.zeros((8, width), F32)
        sums = lax.fori_loop(0, row_count, step, (zero,) * len(pairs))
        lane = lax.broadcasted_iota(jnp.int32, part.shape, 1)
        row_of = part[...]
        for value, (left, right) in zip(sums, pairs):
            whole = jnp.sum(jnp.sum(value, axis=0, keepdims=True), axis=1, keepdims=True)
            row_of = row_of + jnp.where(lane == 3 * left + right, whole, 0.0)
        part[...] = row_of

    part[...] = jnp.zeros(part.shape, F32)

    def pair_copy():
        return pltpu.make_async_remote_copy(
            part, took_pair, sum_send.at[0], sum_recv.at[0], device_id=partner, device_id_type=MESH
        )

    def last_step():
        products([(0, 3), (1, 3), (2, 3)])
        copy = pair_copy()
        copy.start()
        copy.wait_recv()
        part_pair[...] = part[...] + took_pair[...]
        for at, offset in enumerate(offsets):
            pltpu.make_async_remote_copy(
                part_pair, took.at[at], sum_send.at[1], sum_recv.at[1],
                device_id=chip_peer(offset), device_id_type=MESH,
            ).start()
        wait_all(took, sum_recv.at[1])
        sums = part_pair[...] + jnp.sum(took[...], axis=0)

        def gram(left, right):
            at = 3 * left + right
            return sums[:, at : at + 1]

        g00, g01, g02, g03 = (gram(0, at) for at in range(4))
        g11, g12, g13 = (gram(1, at) for at in range(1, 4))
        g22, g23 = gram(2, 2), gram(2, 3)
        s1 = g00 - g01
        k1 = g00 / s1
        rest = 1.0 - k1
        b1, f11 = g01, g11
        b2 = rest * g01 + k1 * g02
        f12 = rest * g11 + k1 * g12
        f2v2 = rest * g12 + k1 * g22
        f22 = rest * f12 + k1 * f2v2
        a1 = b1 - b2
        left1 = k1 * f11 / s1
        s2 = -k1 * (f12 - f11) - left1 * (b2 - b1)
        m2 = k1 - 1.0 - a1 / s1
        c22 = -k1 * f12 - left1 * b2
        alpha = 1.0 - c22 / s2
        beta = b2 / s1 - c22 * m2 / s2
        both = k1 + beta
        h1 = (1.0 - both) - alpha * rest
        h2 = both + alpha * rest - alpha * k1
        h3 = alpha * k1
        b3 = h1 * g01 + h2 * g02 + h3 * g03
        f13 = h1 * g11 + h2 * g12 + h3 * g13
        f23 = rest * f13 + k1 * (h1 * g12 + h2 * g22 + h3 * g23)
        a1 = b2 - b3
        a2 = -k1 * (f13 - f12) - left1 * (b3 - b2)
        l1 = (alpha * f12 + beta * f11) / s1
        l2 = (alpha * (f22 + m2 * f12) + beta * (f12 + m2 * f11)) / s2
        s3 = -(alpha * (f23 - f22) + beta * (f13 - f12)) + l1 * a1 + l2 * a2
        on2 = alpha - 1.0 - a2 / s2
        on1 = beta - a1 / s1 - a2 * m2 / s2
        c1 = -b3
        c2 = -k1 * f13 - left1 * b3
        c3 = -(alpha * f23 + beta * f13) + l1 * c1 + l2 * c2
        w3 = 1.0 - c3 / s3
        w2 = alpha - c2 / s2 - c3 * on2 / s3
        w1 = both - c1 / s1 - c2 * m2 / s2 - c3 * on1 / s3
        y1 = w1 + w2 * rest + w3 * h1
        y2 = w2 * k1 + w3 * h2
        y3 = w3 * h3

        def fill(row, _):
            out[row] = (vecs[0, row] + y1 * vecs[1, row]) + (y2 * vecs[2, row] + y3 * vecs[3, row])
            return 0

        lax.fori_loop(0, row_count, fill, 0)

        def blank(row, _):
            out[row] = jnp.zeros(out.shape[1:], F32)
            return 0

        lax.fori_loop(row_count, full_rows, blank, 0)

    @on(0)
    def _():
        send_halo(0, 0)
        send_rim(0)
        send_terms(0, 0)
        for copy in input_copies(0)[5:]:
            copy.wait()
        prepare(0)

    for level in range(1, BRANCHES):

        @on(level)
        def _(level=level):
            send_rim(level)
            for copy in input_copies(level):
                copy.wait()
            prepare(level)

    def body(turn, _):
        to = turn + 1
        later = turn > 0

        for level in range(BRANCHES):

            @pl.when(jnp.logical_and(branch == level, later))
            def _(level=level):
                send_terms(level, turn)

            @pl.when(jnp.logical_and(branch == level, later if level > 0 else turn >= 0))
            def _(level=level):
                convs_before(level, turn, to)

        @pl.when(turn == 1)
        def _():
            products([(0, 0), (0, 1), (1, 1)])

        @pl.when(turn == 2)
        def _():
            products([(0, 2), (1, 2), (2, 2)])

        for level in range(BRANCHES):

            @pl.when(jnp.logical_and(branch == level, turn == 0))
            def _(level=level):
                wait_rim(level)

            @pl.when(jnp.logical_and(branch == level, later if level > 0 else turn >= 0))
            def _(level=level):
                convs_after(level, turn, to)

            for when in range(ITERS):

                @pl.when(jnp.logical_and(branch == level, turn == when))
                def _(level=level, when=when):
                    finish(level, when)

        return 0

    lax.fori_loop(0, ITERS, body, 0)
    last_step()

    for level in range(BRANCHES):

        @on(level)
        def _(level=level):
            @pl.when(has_below)
            def _():
                rim_copy(level, True).wait_send()

            @pl.when(has_above)
            def _():
                rim_copy(level, False).wait_send()

            for turn in range(0 if level == 0 else 1, ITERS):
                for sends, copy, _ in halo_copies(level, turn):

                    @pl.when(sends)
                    def _(copy=copy):
                        copy.wait_send()

                for other in range(BRANCHES):
                    if other != level:
                        join_copy(level, other, turn).wait_send()

    pair_copy().wait_send()
    wait_all(took, sum_send.at[1])


def on_device(pieces, *args):
    full_rows, chans, width = args[5].shape[2:]
    across = min(4, pieces // 2)
    peers = pieces // 2 * BRANCHES - 1
    classes = args[0].shape[0]
    vmem = pltpu.VMEM

    def band_shape(level):
        size, many = BASE_CH << level, GROUP[level]
        return vmem((2, 3 * many * size, (many + 2) * size), BF16)

    def pair_shape(low, high):
        return vmem((ITERS, full_rows * BASE_CH >> (high - low), width >> high), BF16)

    pairs = [(0, 1), (0, 2), (0, 3), (1, 2), (1, 3), (2, 3)]
    scratch = (
        [
            vmem((classes, full_rows, width), BF16),
            vmem((full_rows, width), jnp.int32),
            vmem((full_rows, width), F32),
            vmem((classes, BASE_CH), BF16),
            vmem((full_rows, chans, width), BF16),
            vmem((full_rows + 2, chans, width), BF16),
            vmem((9, 256, 256), BF16),
            vmem((9, 256, 256), BF16),
            vmem((6, 256, 256), BF16),
        ]
        + [band_shape(level) for level in range(BRANCHES)]
        + [
            vmem((6, 256, 256), BF16),
            vmem((256, 128), BF16),
            vmem((1024, 256), BF16),
            vmem((1024, 128), BF16),
            vmem((128, 256), BF16),
            vmem((256, 1024), BF16),
            vmem((128, 1024), BF16),
            vmem((ITERS, full_rows + 4, chans, width), BF16),
            vmem((full_rows + 2, chans, width), BF16),
            vmem((ITERS + 1, full_rows, chans, width), F32),
        ]
        + [pair_shape(*pair) for pair in pairs] * 2
        + [
            vmem((1, 128), F32),
            vmem((1, 128), F32),
            vmem((1, 128), F32),
            vmem((peers, 1, 128), F32),
            pltpu.SemaphoreType.DMA((12,)),
            pltpu.SemaphoreType.DMA((2,)),
            pltpu.SemaphoreType.DMA((2,)),
            pltpu.SemaphoreType.DMA((ITERS, 4)),
            pltpu.SemaphoreType.DMA((ITERS, 4)),
            pltpu.SemaphoreType.DMA((ITERS, 4)),
            pltpu.SemaphoreType.DMA((ITERS, 4)),
            pltpu.SemaphoreType.DMA((2,)),
            pltpu.SemaphoreType.DMA((2,)),
        ]
    )
    result = pl.pallas_call(
        partial(kernel, pieces, across),
        out_shape=jax.ShapeDtypeStruct((full_rows, chans, width), F32),
        in_specs=[pl.BlockSpec(memory_space=pltpu.HBM)] * 9,
        out_specs=pl.BlockSpec(memory_space=pltpu.VMEM),
        scratch_shapes=scratch,
        compiler_params=pltpu.CompilerParams(
            collective_id=0, has_side_effects=True, vmem_limit_bytes=58 * 1024 * 1024
        ),
    )(*args[:3], args[3].T, *args[4:])
    return result[None, None]


def solution(mesh):
    placed = (
        P(None, "rows", None),
        P("rows", None),
        P("rows", None),
        P(),
        P("branch", "rows", None, None, None),
        P("branch", "rows", None, None, None),
        P("branch", None, None, None),
        P("branch", None, None, None),
        P(),
    )
    return jax.shard_map(
        partial(on_device, mesh.shape["rows"]),
        mesh=mesh,
        in_specs=placed,
        out_specs=P("branch", "rows", None, None, None),
        check_vma=False,
    )
```

```python
from functools import partial

import jax
import jax.numpy as jnp
from jax import lax
from jax.experimental import pallas as pl
from jax.experimental.pallas import tpu as pltpu
from jax.sharding import PartitionSpec as P

BASE_CH = 32
BRANCHES = 4
ITERS = 3
GROUP = (6, 2, 1, 1)
MESH = pl.DeviceIdType.MESH
BF16 = jnp.bfloat16
F32 = jnp.float32


def dot(left, right):
    return jnp.dot(left, right, preferred_element_type=F32)


def dot_nt(left, right):
    return lax.dot_general(left, right, (((1,), (1,)), ((), ())), preferred_element_type=F32)


def iotas(shape):
    return lax.broadcasted_iota(jnp.int32, shape, 0), lax.broadcasted_iota(jnp.int32, shape, 1)


def flags(mask):
    return jnp.where(mask, 1.0, 0.0).astype(BF16)


def shift_cols(values, by):
    width = values.shape[1]
    _, col = iotas(values.shape)
    if by == 1:
        return jnp.where(col == 0, 0.0, pltpu.roll(values, 1, 1))
    return jnp.where(col == width - 1, 0.0, pltpu.roll(values, width - 1, 1))


def wait_all(ref, sem):
    pltpu.make_async_copy(ref, ref, sem).wait()


def kernel(
    pieces,
    across,
    logits,
    labels,
    pixel_weight,
    head_weight,
    deriv_inner,
    deriv_outer,
    conv_inner,
    conv_outer,
    join_weight,
    out,
    s_logits,
    s_labels,
    s_pixel,
    s_head,
    outer,
    inner,
    k_outer,
    k_inner,
    k_join,
    band0,
    band1,
    band2,
    band3,
    mix,
    pool2,
    pool4,
    pool8,
    up2,
    up4,
    up8,
    scaled,
    wmap,
    vecs,
    give01,
    give02,
    give03,
    give12,
    give13,
    give23,
    take01,
    take02,
    take03,
    take12,
    take13,
    take23,
    part,
    took,
    known,
    in_sem,
    rim_send,
    rim_recv,
    halo_send,
    halo_recv,
    join_send,
    join_recv,
    sum_send,
    sum_recv,
):
    piece = lax.axis_index("rows")
    branch = lax.axis_index("branch")
    full_rows, width = outer.shape[0], outer.shape[2]
    row_count = jnp.right_shift(jnp.int32(full_rows), branch)
    bands = (band0, band1, band2, band3)
    gives = {(0, 1): give01, (0, 2): give02, (0, 3): give03, (1, 2): give12, (1, 3): give13, (2, 3): give23}
    takes = {(0, 1): take01, (0, 2): take02, (0, 3): take03, (1, 2): take12, (1, 3): take13, (2, 3): take23}
    has_above = piece > 0
    has_below = piece < pieces - 1
    core, chip_x, chip_z = lax.rem(piece, 2), lax.rem(piece // 2, across), piece // (2 * across)
    deep = pieces // (2 * across)

    def sizes(level):
        return full_rows >> level, BASE_CH << level, width >> level, 1 << level

    def hops(offset):
        far = sum(min(step, size - step) for step, size in zip(offset[1:], (across, deep, BRANCHES)))
        return far + 0.3 * offset[0]

    offsets = [
        (c, x, z, y)
        for c in range(2)
        for x in range(across)
        for z in range(deep)
        for y in range(BRANCHES)
        if c or x or z or y
    ]
    offsets.sort(key=hops, reverse=True)

    def peer(offset):
        c = lax.rem(core + offset[0], 2)
        x = lax.rem(chip_x + offset[1], across)
        z = lax.rem(chip_z + offset[2], deep)
        return ((z * across + x) * 2 + c, lax.rem(branch + offset[3], BRANCHES))

    along_x = [peer((0, step, 0, 0)) for step in range(1, across)]
    along_z = [peer((0, 0, step, 0)) for step in range(1, deep)]
    along_y = [peer((0, 0, 0, step)) for step in range(1, BRANCHES)]
    partner = peer((1, 0, 0, 0))
    near = [(lax.rem(piece + step, pieces), branch) for step in (1, 2, pieces - 2, pieces - 1)]
    greeted = near + along_z + along_y + along_x + [partner]

    def on(level):
        return pl.when(branch == level)

    def input_copies(level):
        rows, chans, _, _ = sizes(level)
        lanes = max(chans, 128)
        pairs = []
        if level == 0:
            pairs += [(logits, s_logits), (labels, s_labels), (pixel_weight, s_pixel), (head_weight, s_head)]
        pairs += [
            (deriv_outer.at[0, 0, pl.ds(0, rows)], outer.at[pl.ds(0, rows)]),
            (conv_outer.at[0, :, pl.ds(0, chans), pl.ds(0, lanes)], k_outer.at[:, pl.ds(0, chans), pl.ds(0, lanes)]),
            (conv_inner.at[0, :, pl.ds(0, chans), pl.ds(0, lanes)], k_inner.at[:, pl.ds(0, chans), pl.ds(0, lanes)]),
            (deriv_inner.at[0, 0, pl.ds(0, rows)], inner.at[pl.ds(1, rows)]),
        ]
        for other in range(level):
            few = BASE_CH << other
            pairs.append((join_weight.at[level, other, pl.ds(0, chans)], k_join.at[other, pl.ds(0, chans)]))
            pairs.append((join_weight.at[other, level, pl.ds(0, few)], k_join.at[3 + other, pl.ds(0, few)]))
        return [pltpu.make_async_copy(src, dst, in_sem.at[at]) for at, (src, dst) in enumerate(pairs)]

    for level in range(BRANCHES):

        @on(level)
        def _(level=level):
            for copy in input_copies(level):
                copy.start()

    barrier = pltpu.get_barrier_semaphore()
    for other in greeted:
        pl.semaphore_signal(barrier, inc=1, device_id=other, device_id_type=MESH)

    for ref, factor in ((pool2, 2), (pool4, 4), (pool8, 8)):
        row, col = iotas(ref.shape)
        ref[...] = flags(row // factor == col)
    for ref, factor in ((up2, 2), (up4, 4), (up8, 8)):
        row, col = iotas(ref.shape)
        ref[...] = flags(row == col // factor)

    @pl.when(jnp.logical_not(has_above))
    def _():
        inner[0] = jnp.zeros(inner.shape[1:], BF16)
        for turn in range(ITERS):
            for slot in (0, 1):
                scaled[turn, slot] = jnp.zeros(inner.shape[1:], BF16)

    for level in range(BRANCHES):
        rows = sizes(level)[0]

        @pl.when(jnp.logical_and(branch == level, jnp.logical_not(has_below)))
        def _(rows=rows):
            inner[rows + 1] = jnp.zeros(inner.shape[1:], BF16)
            for turn in range(ITERS):
                for slot in (rows + 2, rows + 3):
                    scaled[turn, slot] = jnp.zeros(inner.shape[1:], BF16)

    @pl.when(jnp.logical_and(branch == 3, piece == 1))
    def _():
        for turn in range(ITERS):
            scaled[turn, 0] = jnp.zeros(inner.shape[1:], BF16)

    @pl.when(jnp.logical_and(branch == 3, piece == pieces - 2))
    def _():
        for turn in range(ITERS):
            scaled[turn, 4] = jnp.zeros(inner.shape[1:], BF16)

    def shuffle(level):
        chans, factor = BASE_CH << level, 1 << level
        row, col = iotas((chans, chans))
        return flags(col == factor * lax.rem(row, BASE_CH) + row // BASE_CH)

    def prepare(level):
        rows, chans, _, _ = sizes(level)
        many = GROUP[level]
        order = shuffle(level)
        for which, kernels in enumerate((k_outer, k_inner)):
            for dx in range(3):
                taps = [kernels[3 * dy + dx, :chans, :chans] for dy in (2, 1, 0)]
                if level > 0:
                    taps = [dot(order, tap).astype(BF16) for tap in taps]
                line = dot_nt(order, jnp.concatenate(taps, axis=0)).astype(BF16)
                if many == 1:
                    bands[level][which, dx * chans : (dx + 1) * chans, :] = line
                else:
                    for row_out in range(many):
                        at, to = iotas((3 * chans, (many + 2) * chans))
                        placed = dot(line, flags(to == at + row_out * chans))
                        start = (dx * many + row_out) * chans
                        bands[level][which, start : start + chans, :] = placed.astype(BF16)
        for other in range(level):
            few = BASE_CH << other
            sent = dot(order, k_join[other, :chans, :few]).astype(BF16)
            mix[other, :few, :chans] = dot_nt(shuffle(other), sent).astype(BF16)
            got = dot(shuffle(other), k_join[3 + other, :few, :chans]).astype(BF16)
            mix[3 + other, :chans, :few] = dot_nt(order, got).astype(BF16)

    @on(0)
    def _():
        for copy in input_copies(0)[:5]:
            copy.wait()
        scores = s_logits[...].astype(F32)
        powers = jnp.exp(scores - jnp.max(scores, axis=0, keepdims=True))
        shares = powers / jnp.sum(powers, axis=0, keepdims=True)
        classes = lax.broadcasted_iota(jnp.int32, scores.shape, 0)
        hits = jnp.where(s_labels[...][None] == classes, 1.0, 0.0)
        err = s_pixel[...][None] * (shares - hits)
        count = scores.shape[0]
        flat = err.reshape(count * full_rows, width).astype(BF16)
        row, col = iotas((full_rows * BASE_CH, BASE_CH))
        tall = dot_nt(flags(lax.rem(row, BASE_CH) == col), s_head[...]).astype(BF16)
        row, col = iotas((count, count * full_rows))
        wide = dot(tall, flags(row == col // full_rows))
        row, col = iotas(wide.shape)
        head = jnp.where(row // BASE_CH == lax.rem(col, full_rows), wide, 0.0).astype(BF16)
        first = dot(head, flat)
        for row in range(full_rows):
            own = first[row * BASE_CH : (row + 1) * BASE_CH]
            vecs[0, row] = own
            scaled[0, 2 + row] = (outer[row].astype(F32) * own).astype(BF16)

    @pl.when(branch > 0)
    def _():
        def clear(row, _):
            vecs[0, row] = jnp.zeros(vecs.shape[2:], F32)
            return 0

        lax.fori_loop(0, full_rows, clear, 0)

        def blank(row, _):
            out[row] = jnp.zeros(out.shape[1:], F32)
            return 0

        lax.fori_loop(row_count, full_rows, blank, 0)

    pl.semaphore_wait(barrier, len(greeted))

    circles = (along_x, along_y, [partner])

    def tell(at):
        for other in circles[at]:
            pl.semaphore_signal(known.at[at], inc=1, device_id=other, device_id_type=MESH)

    def hear(at):
        pl.semaphore_wait(known.at[at], len(circles[at]))

    tell(0)

    def rim_copy(level, below):
        rows = sizes(level)[0]
        if below:
            return pltpu.make_async_remote_copy(
                deriv_inner.at[0, 0, rows - 1], inner.at[0], rim_send.at[0], rim_recv.at[0],
                device_id=(piece + 1, branch), device_id_type=MESH,
            )
        return pltpu.make_async_remote_copy(
            deriv_inner.at[0, 0, 0], inner.at[rows + 1], rim_send.at[1], rim_recv.at[1],
            device_id=(piece - 1, branch), device_id_type=MESH,
        )

    def send_rim(level):
        @pl.when(has_below)
        def _():
            rim_copy(level, True).start()

        @pl.when(has_above)
        def _():
            rim_copy(level, False).start()

    def wait_rim(level):
        rows = sizes(level)[0]

        @pl.when(has_above)
        def _():
            wait_all(inner.at[0], rim_recv.at[0])

        @pl.when(has_below)
        def _():
            wait_all(inner.at[rows + 1], rim_recv.at[1])

    def halo_copies(level, turn):
        rows = sizes(level)[0]
        if level < 3:
            plan = [
                (1, slice(rows, rows + 2), slice(0, 2)),
                (-1, slice(2, 4), slice(rows + 2, rows + 4)),
            ]
        else:
            plan = [
                (1, slice(2, 3), slice(1, 2)),
                (-1, slice(2, 3), slice(3, 4)),
                (2, slice(2, 3), slice(0, 1)),
                (-2, slice(2, 3), slice(4, 5)),
            ]
        result = []
        for at, (step, src, dst) in enumerate(plan):
            there = piece + step
            source = piece - step
            copy = pltpu.make_async_remote_copy(
                scaled.at[turn, pl.ds(src.start, src.stop - src.start)],
                scaled.at[turn, pl.ds(dst.start, dst.stop - dst.start)],
                halo_send.at[turn, at],
                halo_recv.at[turn, at],
                device_id=(there, branch),
                device_id_type=MESH,
            )
            sends = there < pieces if step > 0 else there >= 0
            gets = source >= 0 if step > 0 else source < pieces
            result.append((sends, copy, gets))
        return result

    def send_halo(level, turn):
        for sends, copy, _ in halo_copies(level, turn):

            @pl.when(sends)
            def _(copy=copy):
                copy.start()

    def join_copy(level, other, turn):
        pair = (min(level, other), max(level, other))
        return pltpu.make_async_remote_copy(
            gives[pair].at[turn], takes[pair].at[turn], join_send.at[turn, other], join_recv.at[turn, level],
            device_id=(piece, jnp.int32(other)), device_id_type=MESH,
        )

    def chunks(block, level):
        span = width >> level
        return [block[:, at * span : (at + 1) * span] for at in range(1 << level)]

    def grid_rows(load, slots, level):
        return jnp.concatenate([part for slot in slots for part in chunks(load(slot), level)], axis=0)

    def send_terms(level, turn):
        rows, chans, cols, _ = sizes(level)
        load = lambda slot: scaled[turn, slot]
        own = grid_rows(load, range(2, 2 + rows), level)
        for other in range(level + 1, BRANCHES):
            factor = 1 << (other - level)
            height, less = rows // factor, cols // factor
            ref = gives[(level, other)]
            if factor == 2:
                spans = [(at, pool2[...]) for at in range(cols // 256)]
                pieces_of = [dot(own[:, at * 256 : (at + 1) * 256], mat) for at, mat in spans]
            else:
                mat = pool4[:cols, :less] if factor == 4 else pool8[:cols, :less]
                pieces_of = [dot(own, mat)]
            for at, part in enumerate(pieces_of):
                span = part.shape[1]
                for row in range(height):
                    summed = part[row * factor * chans : (row * factor + 1) * chans]
                    for extra in range(1, factor):
                        start = (row * factor + extra) * chans
                        summed = summed + part[start : start + chans]
                    ref[turn, row * chans : (row + 1) * chans, at * span : (at + 1) * span] = summed.astype(BF16)
            join_copy(level, other, turn).start()
        for other in range(level):
            few = BASE_CH << other
            factor = 1 << (level - other)
            scale = few ** (-0.5) / (factor * factor)
            ref = gives[(other, level)]
            matrix = mix[other, :few, :chans]
            for row in range(rows):
                mixed = dot(matrix, own[row * chans : (row + 1) * chans])
                ref[turn, row * few : (row + 1) * few, :] = (mixed * scale).astype(BF16)
            join_copy(level, other, turn).start()

    def conv(level, which, load, first, many):
        _, chans, _, _ = sizes(level)
        most = GROUP[level]
        band = bands[level]
        right = grid_rows(load, range(first, first + many + 2), level)
        if many == most:
            left = band[which]
        else:
            left = jnp.concatenate(
                [
                    band[which, dx * most * chans : (dx * most + many) * chans, : (many + 2) * chans]
                    for dx in range(3)
                ],
                axis=0,
            )
        prod = dot(left, right)
        size = many * chans
        return prod[size : 2 * size] + shift_cols(prod[2 * size :], 1) + shift_cols(prod[:size], -1)

    def conv_lanes(level, which, load, first, many):
        _, chans, cols, _ = sizes(level)
        right = jnp.concatenate(
            [grid_rows(load, range(first + at, first + at + 3), level) for at in range(many)], axis=1
        )
        prod = dot(bands[level][which], right)
        result = []
        for at in range(many):
            own = prod[:, at * cols : (at + 1) * cols]
            result.append(
                own[chans : 2 * chans] + shift_cols(own[2 * chans :], 1) + shift_cols(own[:chans], -1)
            )
        return result

    def put_w(level, row, values):
        _, chans, cols, factor = sizes(level)
        scale = (9 * chans) ** (-0.5)
        for at in range(factor):
            lanes = slice(at * cols, (at + 1) * cols)
            part = values[at * BASE_CH : (at + 1) * BASE_CH] * scale
            wmap[row + 1, :, lanes] = (inner[row + 1, :, lanes].astype(F32) * part).astype(BF16)

    def put_out(level, turn, to, row, values):
        _, chans, cols, factor = sizes(level)
        scale = (9 * chans) ** (-0.5)
        for at in range(factor):
            lanes = slice(at * cols, (at + 1) * cols)
            part = values[at * BASE_CH : (at + 1) * BASE_CH] * scale
            vecs[to, row, :, lanes] = scaled[turn, 2 + row, :, lanes].astype(F32) + part

    def outer_conv(level, turn, starts):
        chans = BASE_CH << level
        load = lambda slot: scaled[turn, slot]
        for first, many in starts:
            if level == 3:
                for at, values in enumerate(conv_lanes(level, 0, load, first + 1, many)):
                    put_w(level, first + at, values)
            else:
                values = conv(level, 0, load, first + 1, many)
                for at in range(many):
                    put_w(level, first + at, values[at * chans : (at + 1) * chans])

    def inner_conv(level, turn, to, starts):
        chans = BASE_CH << level
        load = lambda slot: wmap[slot]
        for first, many in starts:
            if level == 3:
                for at, values in enumerate(conv_lanes(level, 1, load, first, many)):
                    put_out(level, turn, to, first + at, values)
            else:
                values = conv(level, 1, load, first, many)
                for at in range(many):
                    put_out(level, turn, to, first + at, values[at * chans : (at + 1) * chans])

    inside = ([(1, 6)], [(1, 2)], [], [])
    edges = ([(-1, 2), (7, 2)], [(-1, 2), (3, 2)], [(-1, 1), (0, 1), (1, 1), (2, 1)], [(-1, 3)])
    early = ([(2, 4)], [], [], [])
    finals = ([(0, 2), (6, 2)], [(0, 2), (2, 2)], [(0, 1), (1, 1)], [(0, 1)])
    order = ((0, 1, 6, 7, 2, 3, 4, 5), (0, 1, 2, 3), (0, 1), (0,))
    rims = (4, 4, 2, 1)

    def convs_before(level, turn, to):
        outer_conv(level, turn, inside[level])
        inner_conv(level, turn, to, early[level])

    def convs_after(level, turn, to):
        for _, copy, gets in halo_copies(level, turn):

            @pl.when(gets)
            def _(copy=copy):
                copy.wait_recv()

        outer_conv(level, turn, edges[level])
        inner_conv(level, turn, to, finals[level])

    def term_rows(level, other, turn):
        rows, chans, cols, _ = sizes(level)
        pair = (min(level, other), max(level, other))
        ref = takes[pair]
        wait_all(ref.at[turn], join_recv.at[turn, other])
        if other < level:
            less = BASE_CH << other
            matrix = mix[3 + other, :chans, :less]
            scale = chans ** (-0.5)
            mixed = [dot(matrix, ref[turn, row * less : (row + 1) * less, :]) for row in range(rows)]
            return [(value * scale).astype(BF16).astype(F32) for value in mixed]
        times = 1 << (other - level)
        got = ref[turn]
        if times == 2:
            wide = jnp.concatenate(
                [dot(got[:, at * 128 : (at + 1) * 128], up2[...]) for at in range(cols // 256)], axis=1
            )
        else:
            wide = dot(got, up4[: cols // 4, :cols] if times == 4 else up8[: cols // 8, :cols])
        starts = [(row // times) * chans for row in range(rows)]
        return [wide[start : start + chans] for start in starts]

    def finish(level, turn):
        _, _, cols, factor = sizes(level)
        to = turn + 1
        others = [other for other in range(BRANCHES) if other != level and (turn > 0 or other == 0)]
        terms = [term_rows(level, other, turn) for other in others]
        for done, row in enumerate(order[level]):
            for at in range(factor):
                lanes = slice(at * cols, (at + 1) * cols)
                parts = [] if level > 0 and turn == 0 else [vecs[to, row, :, lanes]]
                parts += [term[row][at * BASE_CH : (at + 1) * BASE_CH] for term in terms]
                value = parts[0]
                for more in parts[1:]:
                    value = value + more
                vecs[to, row, :, lanes] = value
                if to < ITERS:
                    scaled[to, 2 + row, :, lanes] = (outer[row, :, lanes].astype(F32) * value).astype(BF16)
            if to < ITERS and done + 1 == rims[level]:
                send_halo(level, to)

    def products(pairs):
        def step(row, sums):
            result = []
            for have, (left, right) in zip(sums, pairs):
                prod = vecs[left, row] * vecs[right, row]
                result.append(have + ((prod[0:8] + prod[8:16]) + (prod[16:24] + prod[24:32])))
            return tuple(result)

        zero = jnp.zeros((8, width), F32)
        sums = lax.fori_loop(0, row_count, step, (zero,) * len(pairs))
        lane = lax.broadcasted_iota(jnp.int32, part.shape, 1)
        row_of = part[...]
        for value, (left, right) in zip(sums, pairs):
            whole = jnp.sum(jnp.sum(value, axis=0, keepdims=True), axis=1, keepdims=True)
            row_of = row_of + jnp.where(lane == 3 * left + right, whole, 0.0)
        part[...] = row_of

    part[...] = jnp.zeros(part.shape, F32)

    def last_step():
        products([(0, 3), (1, 3), (2, 3)])
        hear(2)
        for at, offset in enumerate(offsets):
            pltpu.make_async_remote_copy(
                part, took.at[at], sum_send, sum_recv, device_id=peer(offset), device_id_type=MESH
            ).start()
        wait_all(took, sum_recv)
        sums = part[...] + jnp.sum(took[...], axis=0)

        def gram(left, right):
            at = 3 * left + right
            return sums[:, at : at + 1]

        g00, g01, g02, g03 = (gram(0, at) for at in range(4))
        g11, g12, g13 = (gram(1, at) for at in range(1, 4))
        g22, g23 = gram(2, 2), gram(2, 3)
        s1 = g00 - g01
        k1 = g00 / s1
        rest = 1.0 - k1
        b1, f11 = g01, g11
        b2 = rest * g01 + k1 * g02
        f12 = rest * g11 + k1 * g12
        f2v2 = rest * g12 + k1 * g22
        f22 = rest * f12 + k1 * f2v2
        a1 = b1 - b2
        left1 = k1 * f11 / s1
        s2 = -k1 * (f12 - f11) - left1 * (b2 - b1)
        m2 = k1 - 1.0 - a1 / s1
        c22 = -k1 * f12 - left1 * b2
        alpha = 1.0 - c22 / s2
        beta = b2 / s1 - c22 * m2 / s2
        both = k1 + beta
        h1 = (1.0 - both) - alpha * rest
        h2 = both + alpha * rest - alpha * k1
        h3 = alpha * k1
        b3 = h1 * g01 + h2 * g02 + h3 * g03
        f13 = h1 * g11 + h2 * g12 + h3 * g13
        f23 = rest * f13 + k1 * (h1 * g12 + h2 * g22 + h3 * g23)
        a1 = b2 - b3
        a2 = -k1 * (f13 - f12) - left1 * (b3 - b2)
        l1 = (alpha * f12 + beta * f11) / s1
        l2 = (alpha * (f22 + m2 * f12) + beta * (f12 + m2 * f11)) / s2
        s3 = -(alpha * (f23 - f22) + beta * (f13 - f12)) + l1 * a1 + l2 * a2
        on2 = alpha - 1.0 - a2 / s2
        on1 = beta - a1 / s1 - a2 * m2 / s2
        c1 = -b3
        c2 = -k1 * f13 - left1 * b3
        c3 = -(alpha * f23 + beta * f13) + l1 * c1 + l2 * c2
        w3 = 1.0 - c3 / s3
        w2 = alpha - c2 / s2 - c3 * on2 / s3
        w1 = both - c1 / s1 - c2 * m2 / s2 - c3 * on1 / s3
        y1 = w1 + w2 * rest + w3 * h1
        y2 = w2 * k1 + w3 * h2
        y3 = w3 * h3

        def fill(row, _):
            out[row] = (vecs[0, row] + y1 * vecs[1, row]) + (y2 * vecs[2, row] + y3 * vecs[3, row])
            return 0

        lax.fori_loop(0, row_count, fill, 0)

    @on(0)
    def _():
        send_halo(0, 0)
        send_rim(0)
        send_terms(0, 0)
        for copy in input_copies(0)[5:]:
            copy.wait()
        prepare(0)

    for level in range(1, BRANCHES):

        @on(level)
        def _(level=level):
            send_rim(level)
            for copy in input_copies(level):
                copy.wait()
            prepare(level)

    def body(turn, _):
        to = turn + 1
        later = turn > 0

        for at in range(2):

            @pl.when(turn == at + 1)
            def _(at=at):
                hear(at)
                tell(at + 1)

        for level in range(BRANCHES):

            @pl.when(jnp.logical_and(branch == level, later))
            def _(level=level):
                send_terms(level, turn)

            @pl.when(jnp.logical_and(branch == level, later if level > 0 else turn >= 0))
            def _(level=level):
                convs_before(level, turn, to)

        @pl.when(turn == 1)
        def _():
            products([(0, 0), (0, 1), (1, 1)])

        @pl.when(turn == 2)
        def _():
            products([(0, 2), (1, 2), (2, 2)])

        for level in range(BRANCHES):

            @pl.when(jnp.logical_and(branch == level, turn == 0))
            def _(level=level):
                wait_rim(level)

            @pl.when(jnp.logical_and(branch == level, later if level > 0 else turn >= 0))
            def _(level=level):
                convs_after(level, turn, to)

            for when in range(ITERS):

                @pl.when(jnp.logical_and(branch == level, turn == when))
                def _(level=level, when=when):
                    finish(level, when)

        return 0

    lax.fori_loop(0, ITERS, body, 0)
    last_step()

    for level in range(BRANCHES):

        @on(level)
        def _(level=level):
            @pl.when(has_below)
            def _():
                rim_copy(level, True).wait_send()

            @pl.when(has_above)
            def _():
                rim_copy(level, False).wait_send()

            for turn in range(0 if level == 0 else 1, ITERS):
                for sends, copy, _ in halo_copies(level, turn):

                    @pl.when(sends)
                    def _(copy=copy):
                        copy.wait_send()

                for other in range(BRANCHES):
                    if other != level:
                        join_copy(level, other, turn).wait_send()

    wait_all(took, sum_send)


def on_device(pieces, *args):
    full_rows, chans, width = args[5].shape[2:]
    across = min(4, pieces // 2)
    peers = pieces * BRANCHES - 1
    classes = args[0].shape[0]
    vmem = pltpu.VMEM

    def band_shape(level):
        size, many = BASE_CH << level, GROUP[level]
        return vmem((2, 3 * many * size, (many + 2) * size), BF16)

    def pair_shape(low, high):
        return vmem((ITERS, full_rows * BASE_CH >> (high - low), width >> high), BF16)

    pairs = [(0, 1), (0, 2), (0, 3), (1, 2), (1, 3), (2, 3)]
    scratch = (
        [
            vmem((classes, full_rows, width), BF16),
            vmem((full_rows, width), jnp.int32),
            vmem((full_rows, width), F32),
            vmem((classes, BASE_CH), BF16),
            vmem((full_rows, chans, width), BF16),
            vmem((full_rows + 2, chans, width), BF16),
            vmem((9, 256, 256), BF16),
            vmem((9, 256, 256), BF16),
            vmem((6, 256, 256), BF16),
        ]
        + [band_shape(level) for level in range(BRANCHES)]
        + [
            vmem((6, 256, 256), BF16),
            vmem((256, 128), BF16),
            vmem((1024, 256), BF16),
            vmem((1024, 128), BF16),
            vmem((128, 256), BF16),
            vmem((256, 1024), BF16),
            vmem((128, 1024), BF16),
            vmem((ITERS, full_rows + 4, chans, width), BF16),
            vmem((full_rows + 2, chans, width), BF16),
            vmem((ITERS + 1, full_rows, chans, width), F32),
        ]
        + [pair_shape(*pair) for pair in pairs] * 2
        + [
            vmem((1, 128), F32),
            vmem((peers, 1, 128), F32),
            pltpu.SemaphoreType.REGULAR((3,)),
            pltpu.SemaphoreType.DMA((12,)),
            pltpu.SemaphoreType.DMA((2,)),
            pltpu.SemaphoreType.DMA((2,)),
            pltpu.SemaphoreType.DMA((ITERS, 4)),
            pltpu.SemaphoreType.DMA((ITERS, 4)),
            pltpu.SemaphoreType.DMA((ITERS, 4)),
            pltpu.SemaphoreType.DMA((ITERS, 4)),
            pltpu.SemaphoreType.DMA,
            pltpu.SemaphoreType.DMA,
        ]
    )
    result = pl.pallas_call(
        partial(kernel, pieces, across),
        out_shape=jax.ShapeDtypeStruct((full_rows, chans, width), F32),
        in_specs=[pl.BlockSpec(memory_space=pltpu.HBM)] * 9,
        out_specs=pl.BlockSpec(memory_space=pltpu.VMEM),
        scratch_shapes=scratch,
        compiler_params=pltpu.CompilerParams(
            collective_id=0, has_side_effects=True, vmem_limit_bytes=40 * 1024 * 1024
        ),
    )(*[pltpu.with_memory_space_constraint(arg, pltpu.HBM) for arg in (*args[:3], args[3].T, *args[4:])])
    return result[None, None]


def solution(mesh):
    placed = (
        P(None, "rows", None),
        P("rows", None),
        P("rows", None),
        P(),
        P("branch", "rows", None, None, None),
        P("branch", "rows", None, None, None),
        P("branch", None, None, None),
        P("branch", None, None, None),
        P(),
    )
    return jax.shard_map(
        partial(on_device, mesh.shape["rows"]),
        mesh=mesh,
        in_specs=placed,
        out_specs=P("branch", "rows", None, None, None),
        check_vma=False,
    )
```

```python
from functools import partial

import jax
import jax.numpy as jnp
from jax import lax
from jax.experimental import pallas as pl
from jax.experimental.pallas import tpu as pltpu
from jax.sharding import PartitionSpec as P

BASE_CH = 32
BRANCHES = 4
ITERS = 3
GROUP = (6, 2, 1, 1)
MESH = pl.DeviceIdType.MESH
BF16 = jnp.bfloat16
F32 = jnp.float32


def dot(left, right):
    return jnp.dot(left, right, preferred_element_type=F32)


def dot_nt(left, right):
    return lax.dot_general(left, right, (((1,), (1,)), ((), ())), preferred_element_type=F32)


def iotas(shape):
    return lax.broadcasted_iota(jnp.int32, shape, 0), lax.broadcasted_iota(jnp.int32, shape, 1)


def flags(mask):
    return jnp.where(mask, 1.0, 0.0).astype(BF16)


def shift_cols(values, by):
    width = values.shape[1]
    _, col = iotas(values.shape)
    if by == 1:
        return jnp.where(col == 0, 0.0, pltpu.roll(values, 1, 1))
    return jnp.where(col == width - 1, 0.0, pltpu.roll(values, width - 1, 1))


def wait_all(ref, sem):
    pltpu.make_async_copy(ref, ref, sem).wait()


def kernel(
    pieces,
    across,
    logits,
    labels,
    pixel_weight,
    head_weight,
    deriv_inner,
    deriv_outer,
    conv_inner,
    conv_outer,
    join_weight,
    out,
    s_logits,
    s_labels,
    s_pixel,
    s_head,
    outer,
    inner,
    k_outer,
    k_inner,
    k_join,
    band0,
    band1,
    band2,
    band3,
    mix,
    pool2,
    pool4,
    pool8,
    up2,
    up4,
    up8,
    scaled,
    wmap,
    vecs,
    give01,
    give02,
    give03,
    give12,
    give13,
    give23,
    take01,
    take02,
    take03,
    take12,
    take13,
    take23,
    part,
    took,
    known,
    in_sem,
    rim_send,
    rim_recv,
    halo_send,
    halo_recv,
    join_send,
    join_recv,
    sum_send,
    sum_recv,
):
    piece = lax.axis_index("rows")
    branch = lax.axis_index("branch")
    full_rows, width = outer.shape[0], outer.shape[2]
    row_count = jnp.right_shift(jnp.int32(full_rows), branch)
    bands = (band0, band1, band2, band3)
    gives = {(0, 1): give01, (0, 2): give02, (0, 3): give03, (1, 2): give12, (1, 3): give13, (2, 3): give23}
    takes = {(0, 1): take01, (0, 2): take02, (0, 3): take03, (1, 2): take12, (1, 3): take13, (2, 3): take23}
    has_above = piece > 0
    has_below = piece < pieces - 1
    core, chip_x, chip_z = lax.rem(piece, 2), lax.rem(piece // 2, across), piece // (2 * across)
    deep = pieces // (2 * across)

    def sizes(level):
        return full_rows >> level, BASE_CH << level, width >> level, 1 << level

    spread = [(there, level) for there in range(pieces) for level in range(BRANCHES)]
    spread.sort(key=lambda at: at[0] // (2 * across) + 0.7 * (at[0] // 2 % across) + at[1])
    others = took.at[pl.ds(0, pieces * BRANCHES - 1)]

    def peer(offset):
        c = lax.rem(core + offset[0], 2)
        x = lax.rem(chip_x + offset[1], across)
        z = lax.rem(chip_z + offset[2], deep)
        return ((z * across + x) * 2 + c, lax.rem(branch + offset[3], BRANCHES))

    along_x = [peer((0, step, 0, 0)) for step in range(1, across)]
    along_z = [peer((0, 0, step, 0)) for step in range(1, deep)]
    along_y = [peer((0, 0, 0, step)) for step in range(1, BRANCHES)]
    partner = peer((1, 0, 0, 0))
    near = [(lax.rem(piece + step, pieces), branch) for step in (1, 2, pieces - 2, pieces - 1)]
    greeted = near + along_z + along_y + along_x + [partner]

    def on(level):
        return pl.when(branch == level)

    def input_copies(level):
        rows, chans, _, _ = sizes(level)
        lanes = max(chans, 128)
        pairs = []
        if level == 0:
            pairs += [(logits, s_logits), (labels, s_labels), (pixel_weight, s_pixel), (head_weight, s_head)]
        pairs += [
            (deriv_outer.at[0, 0, pl.ds(0, rows)], outer.at[pl.ds(0, rows)]),
            (conv_outer.at[0, :, pl.ds(0, chans), pl.ds(0, lanes)], k_outer.at[:, pl.ds(0, chans), pl.ds(0, lanes)]),
            (conv_inner.at[0, :, pl.ds(0, chans), pl.ds(0, lanes)], k_inner.at[:, pl.ds(0, chans), pl.ds(0, lanes)]),
            (deriv_inner.at[0, 0, pl.ds(0, rows)], inner.at[pl.ds(1, rows)]),
        ]
        for other in range(level):
            few = BASE_CH << other
            pairs.append((join_weight.at[level, other, pl.ds(0, chans)], k_join.at[other, pl.ds(0, chans)]))
            pairs.append((join_weight.at[other, level, pl.ds(0, few)], k_join.at[3 + other, pl.ds(0, few)]))
        return [pltpu.make_async_copy(src, dst, in_sem.at[at]) for at, (src, dst) in enumerate(pairs)]

    for level in range(BRANCHES):

        @on(level)
        def _(level=level):
            for copy in input_copies(level):
                copy.start()

    barrier = pltpu.get_barrier_semaphore()
    for other in greeted:
        pl.semaphore_signal(barrier, inc=1, device_id=other, device_id_type=MESH)

    for ref, factor in ((pool2, 2), (pool4, 4), (pool8, 8)):
        row, col = iotas(ref.shape)
        ref[...] = flags(row // factor == col)
    for ref, factor in ((up2, 2), (up4, 4), (up8, 8)):
        row, col = iotas(ref.shape)
        ref[...] = flags(row == col // factor)

    @pl.when(jnp.logical_not(has_above))
    def _():
        inner[0] = jnp.zeros(inner.shape[1:], BF16)
        for turn in range(ITERS):
            for slot in (0, 1):
                scaled[turn, slot] = jnp.zeros(inner.shape[1:], BF16)

    for level in range(BRANCHES):
        rows = sizes(level)[0]

        @pl.when(jnp.logical_and(branch == level, jnp.logical_not(has_below)))
        def _(rows=rows):
            inner[rows + 1] = jnp.zeros(inner.shape[1:], BF16)
            for turn in range(ITERS):
                for slot in (rows + 2, rows + 3):
                    scaled[turn, slot] = jnp.zeros(inner.shape[1:], BF16)

    @pl.when(jnp.logical_and(branch == 3, piece == 1))
    def _():
        for turn in range(ITERS):
            scaled[turn, 0] = jnp.zeros(inner.shape[1:], BF16)

    @pl.when(jnp.logical_and(branch == 3, piece == pieces - 2))
    def _():
        for turn in range(ITERS):
            scaled[turn, 4] = jnp.zeros(inner.shape[1:], BF16)

    def shuffle(level):
        chans, factor = BASE_CH << level, 1 << level
        row, col = iotas((chans, chans))
        return flags(col == factor * lax.rem(row, BASE_CH) + row // BASE_CH)

    def prepare(level):
        rows, chans, _, _ = sizes(level)
        many = GROUP[level]
        order = shuffle(level)
        for which, kernels in enumerate((k_outer, k_inner)):
            for dx in range(3):
                taps = [kernels[3 * dy + dx, :chans, :chans] for dy in (2, 1, 0)]
                if level > 0:
                    taps = [dot(order, tap).astype(BF16) for tap in taps]
                line = dot_nt(order, jnp.concatenate(taps, axis=0)).astype(BF16)
                if many == 1:
                    bands[level][which, dx * chans : (dx + 1) * chans, :] = line
                else:
                    for row_out in range(many):
                        at, to = iotas((3 * chans, (many + 2) * chans))
                        placed = dot(line, flags(to == at + row_out * chans))
                        start = (dx * many + row_out) * chans
                        bands[level][which, start : start + chans, :] = placed.astype(BF16)
        for other in range(level):
            few = BASE_CH << other
            sent = dot(order, k_join[other, :chans, :few]).astype(BF16)
            mix[other, :few, :chans] = dot_nt(shuffle(other), sent).astype(BF16)
            got = dot(shuffle(other), k_join[3 + other, :few, :chans]).astype(BF16)
            mix[3 + other, :chans, :few] = dot_nt(order, got).astype(BF16)

    @on(0)
    def _():
        for copy in input_copies(0)[:5]:
            copy.wait()
        scores = s_logits[...].astype(F32)
        powers = jnp.exp(scores - jnp.max(scores, axis=0, keepdims=True))
        shares = powers / jnp.sum(powers, axis=0, keepdims=True)
        classes = lax.broadcasted_iota(jnp.int32, scores.shape, 0)
        hits = jnp.where(s_labels[...][None] == classes, 1.0, 0.0)
        err = s_pixel[...][None] * (shares - hits)
        count = scores.shape[0]
        flat = err.reshape(count * full_rows, width).astype(BF16)
        row, col = iotas((full_rows * BASE_CH, BASE_CH))
        tall = dot_nt(flags(lax.rem(row, BASE_CH) == col), s_head[...]).astype(BF16)
        row, col = iotas((count, count * full_rows))
        wide = dot(tall, flags(row == col // full_rows))
        row, col = iotas(wide.shape)
        head = jnp.where(row // BASE_CH == lax.rem(col, full_rows), wide, 0.0).astype(BF16)
        first = dot(head, flat)
        for row in range(full_rows):
            own = first[row * BASE_CH : (row + 1) * BASE_CH]
            vecs[0, row] = own
            scaled[0, 2 + row] = (outer[row].astype(F32) * own).astype(BF16)

    @pl.when(branch > 0)
    def _():
        def clear(row, _):
            vecs[0, row] = jnp.zeros(vecs.shape[2:], F32)
            return 0

        lax.fori_loop(0, full_rows, clear, 0)

        def blank(row, _):
            out[row] = jnp.zeros(out.shape[1:], F32)
            return 0

        lax.fori_loop(row_count, full_rows, blank, 0)

    pl.semaphore_wait(barrier, len(greeted))

    circles = (along_x, along_y, [partner])

    def tell(at):
        for other in circles[at]:
            pl.semaphore_signal(known.at[at], inc=1, device_id=other, device_id_type=MESH)

    def hear(at):
        pl.semaphore_wait(known.at[at], len(circles[at]))

    tell(0)

    def rim_copy(level, below):
        rows = sizes(level)[0]
        if below:
            return pltpu.make_async_remote_copy(
                deriv_inner.at[0, 0, rows - 1], inner.at[0], rim_send.at[0], rim_recv.at[0],
                device_id=(piece + 1, branch), device_id_type=MESH,
            )
        return pltpu.make_async_remote_copy(
            deriv_inner.at[0, 0, 0], inner.at[rows + 1], rim_send.at[1], rim_recv.at[1],
            device_id=(piece - 1, branch), device_id_type=MESH,
        )

    def send_rim(level):
        @pl.when(has_below)
        def _():
            rim_copy(level, True).start()

        @pl.when(has_above)
        def _():
            rim_copy(level, False).start()

    def wait_rim(level):
        rows = sizes(level)[0]

        @pl.when(has_above)
        def _():
            wait_all(inner.at[0], rim_recv.at[0])

        @pl.when(has_below)
        def _():
            wait_all(inner.at[rows + 1], rim_recv.at[1])

    def halo_copies(level, turn):
        rows = sizes(level)[0]
        if level < 3:
            plan = [
                (1, slice(rows, rows + 2), slice(0, 2)),
                (-1, slice(2, 4), slice(rows + 2, rows + 4)),
            ]
        else:
            plan = [
                (1, slice(2, 3), slice(1, 2)),
                (-1, slice(2, 3), slice(3, 4)),
                (2, slice(2, 3), slice(0, 1)),
                (-2, slice(2, 3), slice(4, 5)),
            ]
        result = []
        for at, (step, src, dst) in enumerate(plan):
            there = piece + step
            source = piece - step
            copy = pltpu.make_async_remote_copy(
                scaled.at[turn, pl.ds(src.start, src.stop - src.start)],
                scaled.at[turn, pl.ds(dst.start, dst.stop - dst.start)],
                halo_send.at[turn, at],
                halo_recv.at[turn, at],
                device_id=(there, branch),
                device_id_type=MESH,
            )
            sends = there < pieces if step > 0 else there >= 0
            gets = source >= 0 if step > 0 else source < pieces
            result.append((sends, copy, gets))
        return result

    def send_halo(level, turn):
        for sends, copy, _ in halo_copies(level, turn):

            @pl.when(sends)
            def _(copy=copy):
                copy.start()

    def join_copy(level, other, turn):
        pair = (min(level, other), max(level, other))
        return pltpu.make_async_remote_copy(
            gives[pair].at[turn], takes[pair].at[turn], join_send.at[turn, other], join_recv.at[turn, level],
            device_id=(piece, jnp.int32(other)), device_id_type=MESH,
        )

    def chunks(block, level):
        span = width >> level
        return [block[:, at * span : (at + 1) * span] for at in range(1 << level)]

    def grid_rows(load, slots, level):
        return jnp.concatenate([part for slot in slots for part in chunks(load(slot), level)], axis=0)

    def send_terms(level, turn, coarser=None):
        rows, chans, cols, _ = sizes(level)
        load = lambda slot: scaled[turn, slot]
        own = grid_rows(load, range(2, 2 + rows), level)
        for other in coarser or range(level + 1, BRANCHES):
            factor = 1 << (other - level)
            height, less = rows // factor, cols // factor
            ref = gives[(level, other)]
            if factor == 2:
                spans = [(at, pool2[...]) for at in range(cols // 256)]
                pieces_of = [dot(own[:, at * 256 : (at + 1) * 256], mat) for at, mat in spans]
            else:
                mat = pool4[:cols, :less] if factor == 4 else pool8[:cols, :less]
                pieces_of = [dot(own, mat)]
            for at, part in enumerate(pieces_of):
                span = part.shape[1]
                for row in range(height):
                    summed = part[row * factor * chans : (row * factor + 1) * chans]
                    for extra in range(1, factor):
                        start = (row * factor + extra) * chans
                        summed = summed + part[start : start + chans]
                    ref[turn, row * chans : (row + 1) * chans, at * span : (at + 1) * span] = summed.astype(BF16)
            join_copy(level, other, turn).start()
        for other in range(level):
            few = BASE_CH << other
            factor = 1 << (level - other)
            scale = few ** (-0.5) / (factor * factor)
            ref = gives[(other, level)]
            matrix = mix[other, :few, :chans]
            for row in range(rows):
                mixed = dot(matrix, own[row * chans : (row + 1) * chans])
                ref[turn, row * few : (row + 1) * few, :] = (mixed * scale).astype(BF16)
            join_copy(level, other, turn).start()

    def conv(level, which, load, first, many):
        _, chans, _, _ = sizes(level)
        most = GROUP[level]
        band = bands[level]
        right = grid_rows(load, range(first, first + many + 2), level)
        if many == most:
            left = band[which]
        else:
            left = jnp.concatenate(
                [
                    band[which, dx * most * chans : (dx * most + many) * chans, : (many + 2) * chans]
                    for dx in range(3)
                ],
                axis=0,
            )
        prod = dot(left, right)
        size = many * chans
        return prod[size : 2 * size] + shift_cols(prod[2 * size :], 1) + shift_cols(prod[:size], -1)

    def conv_lanes(level, which, load, first, many):
        _, chans, cols, _ = sizes(level)
        right = jnp.concatenate(
            [grid_rows(load, range(first + at, first + at + 3), level) for at in range(many)], axis=1
        )
        prod = dot(bands[level][which], right)
        result = []
        for at in range(many):
            own = prod[:, at * cols : (at + 1) * cols]
            result.append(
                own[chans : 2 * chans] + shift_cols(own[2 * chans :], 1) + shift_cols(own[:chans], -1)
            )
        return result

    def put_w(level, row, values):
        _, chans, cols, factor = sizes(level)
        scale = (9 * chans) ** (-0.5)
        for at in range(factor):
            lanes = slice(at * cols, (at + 1) * cols)
            part = values[at * BASE_CH : (at + 1) * BASE_CH] * scale
            wmap[row + 1, :, lanes] = (inner[row + 1, :, lanes].astype(F32) * part).astype(BF16)

    def put_out(level, turn, to, row, values):
        _, chans, cols, factor = sizes(level)
        scale = (9 * chans) ** (-0.5)
        for at in range(factor):
            lanes = slice(at * cols, (at + 1) * cols)
            part = values[at * BASE_CH : (at + 1) * BASE_CH] * scale
            vecs[to, row, :, lanes] = scaled[turn, 2 + row, :, lanes].astype(F32) + part

    def outer_conv(level, turn, starts):
        chans = BASE_CH << level
        load = lambda slot: scaled[turn, slot]
        for first, many in starts:
            if level == 3:
                for at, values in enumerate(conv_lanes(level, 0, load, first + 1, many)):
                    put_w(level, first + at, values)
            else:
                values = conv(level, 0, load, first + 1, many)
                for at in range(many):
                    put_w(level, first + at, values[at * chans : (at + 1) * chans])

    def inner_conv(level, turn, to, starts):
        chans = BASE_CH << level
        load = lambda slot: wmap[slot]
        for first, many in starts:
            if level == 3:
                for at, values in enumerate(conv_lanes(level, 1, load, first, many)):
                    put_out(level, turn, to, first + at, values)
            else:
                values = conv(level, 1, load, first, many)
                for at in range(many):
                    put_out(level, turn, to, first + at, values[at * chans : (at + 1) * chans])

    inside = ([(1, 6)], [(1, 2)], [], [])
    edges = ([(-1, 2), (7, 2)], [(-1, 2), (3, 2)], [(-1, 1), (0, 1), (1, 1), (2, 1)], [(-1, 3)])
    early = ([(2, 4)], [], [], [])
    finals = ([(0, 2), (6, 2)], [(0, 2), (2, 2)], [(0, 1), (1, 1)], [(0, 1)])
    order = ((0, 1, 6, 7, 2, 3, 4, 5), (0, 1, 2, 3), (0, 1), (0,))
    rims = (4, 4, 2, 1)

    def convs_before(level, turn, to):
        outer_conv(level, turn, inside[level])
        inner_conv(level, turn, to, early[level])

    def convs_after(level, turn, to):
        for _, copy, gets in halo_copies(level, turn):

            @pl.when(gets)
            def _(copy=copy):
                copy.wait_recv()

        outer_conv(level, turn, edges[level])
        inner_conv(level, turn, to, finals[level])

    def term_rows(level, other, turn):
        rows, chans, cols, _ = sizes(level)
        pair = (min(level, other), max(level, other))
        ref = takes[pair]
        wait_all(ref.at[turn], join_recv.at[turn, other])
        if other < level:
            less = BASE_CH << other
            matrix = mix[3 + other, :chans, :less]
            scale = chans ** (-0.5)
            mixed = [dot(matrix, ref[turn, row * less : (row + 1) * less, :]) for row in range(rows)]
            return [(value * scale).astype(BF16).astype(F32) for value in mixed]
        times = 1 << (other - level)
        got = ref[turn]
        if times == 2:
            wide = jnp.concatenate(
                [dot(got[:, at * 128 : (at + 1) * 128], up2[...]) for at in range(cols // 256)], axis=1
            )
        else:
            wide = dot(got, up4[: cols // 4, :cols] if times == 4 else up8[: cols // 8, :cols])
        starts = [(row // times) * chans for row in range(rows)]
        return [wide[start : start + chans] for start in starts]

    def finish(level, turn):
        _, _, cols, factor = sizes(level)
        to = turn + 1
        others = [other for other in range(BRANCHES) if other != level and (turn > 0 or other == 0)]
        terms = [term_rows(level, other, turn) for other in others]
        for done, row in enumerate(order[level]):
            for at in range(factor):
                lanes = slice(at * cols, (at + 1) * cols)
                parts = [] if level > 0 and turn == 0 else [vecs[to, row, :, lanes]]
                parts += [term[row][at * BASE_CH : (at + 1) * BASE_CH] for term in terms]
                value = parts[0]
                for more in parts[1:]:
                    value = value + more
                vecs[to, row, :, lanes] = value
                if to < ITERS:
                    scaled[to, 2 + row, :, lanes] = (outer[row, :, lanes].astype(F32) * value).astype(BF16)
            if to < ITERS and done + 1 == rims[level]:
                send_halo(level, to)

    def products(pairs):
        def step(row, sums):
            result = []
            for have, (left, right) in zip(sums, pairs):
                prod = vecs[left, row] * vecs[right, row]
                result.append(have + ((prod[0:8] + prod[8:16]) + (prod[16:24] + prod[24:32])))
            return tuple(result)

        zero = jnp.zeros((8, width), F32)
        sums = lax.fori_loop(0, row_count, step, (zero,) * len(pairs))
        lane = lax.broadcasted_iota(jnp.int32, part.shape, 1)
        row_of = part[...]
        for value, (left, right) in zip(sums, pairs):
            whole = jnp.sum(jnp.sum(value, axis=0, keepdims=True), axis=1, keepdims=True)
            row_of = row_of + jnp.where(lane == 3 * left + right, whole, 0.0)
        part[...] = row_of

    part[...] = jnp.zeros(part.shape, F32)

    def last_step():
        products([(0, 3), (1, 3), (2, 3)])
        hear(2)
        mine = piece * BRANCHES + branch
        for there, level in spread:

            @pl.when(jnp.logical_or(piece != there, branch != level))
            def _(there=there, level=level):
                pltpu.make_async_remote_copy(
                    part, took.at[mine], sum_send, sum_recv,
                    device_id=(jnp.int32(there), jnp.int32(level)), device_id_type=MESH,
                ).start()

        wait_all(others, sum_recv)
        took[mine] = part[...]
        sums = jnp.sum(took[...], axis=0)

        def gram(left, right):
            at = 3 * left + right
            return sums[:, at : at + 1]

        g00, g01, g02, g03 = (gram(0, at) for at in range(4))
        g11, g12, g13 = (gram(1, at) for at in range(1, 4))
        g22, g23 = gram(2, 2), gram(2, 3)
        s1 = g00 - g01
        k1 = g00 / s1
        rest = 1.0 - k1
        b1, f11 = g01, g11
        b2 = rest * g01 + k1 * g02
        f12 = rest * g11 + k1 * g12
        f2v2 = rest * g12 + k1 * g22
        f22 = rest * f12 + k1 * f2v2
        a1 = b1 - b2
        left1 = k1 * f11 / s1
        s2 = -k1 * (f12 - f11) - left1 * (b2 - b1)
        m2 = k1 - 1.0 - a1 / s1
        c22 = -k1 * f12 - left1 * b2
        alpha = 1.0 - c22 / s2
        beta = b2 / s1 - c22 * m2 / s2
        both = k1 + beta
        h1 = (1.0 - both) - alpha * rest
        h2 = both + alpha * rest - alpha * k1
        h3 = alpha * k1
        b3 = h1 * g01 + h2 * g02 + h3 * g03
        f13 = h1 * g11 + h2 * g12 + h3 * g13
        f23 = rest * f13 + k1 * (h1 * g12 + h2 * g22 + h3 * g23)
        a1 = b2 - b3
        a2 = -k1 * (f13 - f12) - left1 * (b3 - b2)
        l1 = (alpha * f12 + beta * f11) / s1
        l2 = (alpha * (f22 + m2 * f12) + beta * (f12 + m2 * f11)) / s2
        s3 = -(alpha * (f23 - f22) + beta * (f13 - f12)) + l1 * a1 + l2 * a2
        on2 = alpha - 1.0 - a2 / s2
        on1 = beta - a1 / s1 - a2 * m2 / s2
        c1 = -b3
        c2 = -k1 * f13 - left1 * b3
        c3 = -(alpha * f23 + beta * f13) + l1 * c1 + l2 * c2
        w3 = 1.0 - c3 / s3
        w2 = alpha - c2 / s2 - c3 * on2 / s3
        w1 = both - c1 / s1 - c2 * m2 / s2 - c3 * on1 / s3
        y1 = w1 + w2 * rest + w3 * h1
        y2 = w2 * k1 + w3 * h2
        y3 = w3 * h3

        def fill(row, _):
            out[row] = (vecs[0, row] + y1 * vecs[1, row]) + (y2 * vecs[2, row] + y3 * vecs[3, row])
            return 0

        lax.fori_loop(0, row_count, fill, 0)

    @on(0)
    def _():
        send_halo(0, 0)
        send_terms(0, 0, (3, 2, 1))
        send_rim(0)
        for copy in input_copies(0)[5:]:
            copy.wait()
        prepare(0)

    for level in range(1, BRANCHES):

        @on(level)
        def _(level=level):
            send_rim(level)
            for copy in input_copies(level):
                copy.wait()
            prepare(level)

    def body(turn, _):
        to = turn + 1
        later = turn > 0

        for at in range(2):

            @pl.when(turn == at + 1)
            def _(at=at):
                hear(at)
                tell(at + 1)

        for level in range(BRANCHES):

            @pl.when(jnp.logical_and(branch == level, later))
            def _(level=level):
                send_terms(level, turn)

            @pl.when(jnp.logical_and(branch == level, later if level > 0 else turn >= 0))
            def _(level=level):
                convs_before(level, turn, to)

        @pl.when(turn == 1)
        def _():
            products([(0, 0), (0, 1), (1, 1)])

        @pl.when(turn == 2)
        def _():
            products([(0, 2), (1, 2), (2, 2)])

        for level in range(BRANCHES):

            @pl.when(jnp.logical_and(branch == level, turn == 0))
            def _(level=level):
                wait_rim(level)

            @pl.when(jnp.logical_and(branch == level, later if level > 0 else turn >= 0))
            def _(level=level):
                convs_after(level, turn, to)

            for when in range(ITERS):

                @pl.when(jnp.logical_and(branch == level, turn == when))
                def _(level=level, when=when):
                    finish(level, when)

        return 0

    lax.fori_loop(0, ITERS, body, 0)
    last_step()

    for level in range(BRANCHES):

        @on(level)
        def _(level=level):
            @pl.when(has_below)
            def _():
                rim_copy(level, True).wait_send()

            @pl.when(has_above)
            def _():
                rim_copy(level, False).wait_send()

            for turn in range(0 if level == 0 else 1, ITERS):
                for sends, copy, _ in halo_copies(level, turn):

                    @pl.when(sends)
                    def _(copy=copy):
                        copy.wait_send()

                for other in range(BRANCHES):
                    if other != level:
                        join_copy(level, other, turn).wait_send()

    wait_all(others, sum_send)


def on_device(pieces, *args):
    full_rows, chans, width = args[5].shape[2:]
    across = min(4, pieces // 2)
    classes = args[0].shape[0]
    vmem = pltpu.VMEM

    def band_shape(level):
        size, many = BASE_CH << level, GROUP[level]
        return vmem((2, 3 * many * size, (many + 2) * size), BF16)

    def pair_shape(low, high):
        return vmem((ITERS, full_rows * BASE_CH >> (high - low), width >> high), BF16)

    pairs = [(0, 1), (0, 2), (0, 3), (1, 2), (1, 3), (2, 3)]
    scratch = (
        [
            vmem((classes, full_rows, width), BF16),
            vmem((full_rows, width), jnp.int32),
            vmem((full_rows, width), F32),
            vmem((classes, BASE_CH), BF16),
            vmem((full_rows, chans, width), BF16),
            vmem((full_rows + 2, chans, width), BF16),
            vmem((9, 256, 256), BF16),
            vmem((9, 256, 256), BF16),
            vmem((6, 256, 256), BF16),
        ]
        + [band_shape(level) for level in range(BRANCHES)]
        + [
            vmem((6, 256, 256), BF16),
            vmem((256, 128), BF16),
            vmem((1024, 256), BF16),
            vmem((1024, 128), BF16),
            vmem((128, 256), BF16),
            vmem((256, 1024), BF16),
            vmem((128, 1024), BF16),
            vmem((ITERS, full_rows + 4, chans, width), BF16),
            vmem((full_rows + 2, chans, width), BF16),
            vmem((ITERS + 1, full_rows, chans, width), F32),
        ]
        + [pair_shape(*pair) for pair in pairs] * 2
        + [
            vmem((1, 128), F32),
            vmem((pieces * BRANCHES, 1, 128), F32),
            pltpu.SemaphoreType.REGULAR((3,)),
            pltpu.SemaphoreType.DMA((12,)),
            pltpu.SemaphoreType.DMA((2,)),
            pltpu.SemaphoreType.DMA((2,)),
            pltpu.SemaphoreType.DMA((ITERS, 4)),
            pltpu.SemaphoreType.DMA((ITERS, 4)),
            pltpu.SemaphoreType.DMA((ITERS, 4)),
            pltpu.SemaphoreType.DMA((ITERS, 4)),
            pltpu.SemaphoreType.DMA,
            pltpu.SemaphoreType.DMA,
        ]
    )
    result = pl.pallas_call(
        partial(kernel, pieces, across),
        out_shape=jax.ShapeDtypeStruct((full_rows, chans, width), F32),
        in_specs=[pl.BlockSpec(memory_space=pltpu.HBM)] * 9,
        out_specs=pl.BlockSpec(memory_space=pltpu.VMEM),
        scratch_shapes=scratch,
        compiler_params=pltpu.CompilerParams(
            collective_id=0, has_side_effects=True, vmem_limit_bytes=40 * 1024 * 1024
        ),
    )(*[pltpu.with_memory_space_constraint(arg, pltpu.HBM) for arg in (*args[:3], args[3].T, *args[4:])])
    return result[None, None]


def solution(mesh):
    placed = (
        P(None, "rows", None),
        P("rows", None),
        P("rows", None),
        P(),
        P("branch", "rows", None, None, None),
        P("branch", "rows", None, None, None),
        P("branch", None, None, None),
        P("branch", None, None, None),
        P(),
    )
    return jax.shard_map(
        partial(on_device, mesh.shape["rows"]),
        mesh=mesh,
        in_specs=placed,
        out_specs=P("branch", "rows", None, None, None),
        check_vma=False,
    )
```

```python
from functools import partial

import jax
import jax.numpy as jnp
from jax import lax
from jax.experimental import pallas as pl
from jax.experimental.pallas import tpu as pltpu
from jax.sharding import PartitionSpec as P

BASE_CH = 32
BRANCHES = 4
ITERS = 3
GROUP = (6, 2, 1, 1)
MESH = pl.DeviceIdType.MESH
BF16 = jnp.bfloat16
F32 = jnp.float32


def dot(left, right):
    return jnp.dot(left, right, preferred_element_type=F32)


def dot_nt(left, right):
    return lax.dot_general(left, right, (((1,), (1,)), ((), ())), preferred_element_type=F32)


def iotas(shape):
    return lax.broadcasted_iota(jnp.int32, shape, 0), lax.broadcasted_iota(jnp.int32, shape, 1)


def flags(mask):
    return jnp.where(mask, 1.0, 0.0).astype(BF16)


def shift_cols(values, by):
    width = values.shape[1]
    _, col = iotas(values.shape)
    if by == 1:
        return jnp.where(col == 0, 0.0, pltpu.roll(values, 1, 1))
    return jnp.where(col == width - 1, 0.0, pltpu.roll(values, width - 1, 1))


def wait_all(ref, sem):
    pltpu.make_async_copy(ref, ref, sem).wait()


def kernel(
    pieces,
    across,
    logits,
    labels,
    pixel_weight,
    head_weight,
    deriv_inner,
    deriv_outer,
    conv_inner,
    conv_outer,
    join_weight,
    out,
    s_logits,
    s_labels,
    s_pixel,
    s_head,
    outer,
    inner,
    k_outer,
    k_inner,
    k_join,
    band0,
    band1,
    band2,
    band3,
    mix,
    pool2,
    pool4,
    pool8,
    up2,
    up4,
    up8,
    scaled,
    wmap,
    vecs,
    give01,
    give02,
    give03,
    give12,
    give13,
    give23,
    take01,
    take02,
    take03,
    take12,
    take13,
    take23,
    part,
    took,
    known,
    in_sem,
    rim_send,
    rim_recv,
    halo_send,
    halo_recv,
    join_send,
    join_recv,
    sum_send,
    sum_recv,
):
    piece = lax.axis_index("rows")
    branch = lax.axis_index("branch")
    full_rows, width = outer.shape[0], outer.shape[2]
    row_count = jnp.right_shift(jnp.int32(full_rows), branch)
    bands = (band0, band1, band2, band3)
    gives = {(0, 1): give01, (0, 2): give02, (0, 3): give03, (1, 2): give12, (1, 3): give13, (2, 3): give23}
    takes = {(0, 1): take01, (0, 2): take02, (0, 3): take03, (1, 2): take12, (1, 3): take13, (2, 3): take23}
    has_above = piece > 0
    has_below = piece < pieces - 1
    core, chip_x, chip_z = lax.rem(piece, 2), lax.rem(piece // 2, across), piece // (2 * across)
    deep = pieces // (2 * across)

    def sizes(level):
        return full_rows >> level, BASE_CH << level, width >> level, 1 << level

    spread = [(there, level) for there in range(pieces) for level in range(BRANCHES)]
    spread.sort(key=lambda at: at[0] // (2 * across) + 0.7 * (at[0] // 2 % across) + at[1])
    others = took.at[pl.ds(0, pieces * BRANCHES - 1)]

    def peer(offset):
        c = lax.rem(core + offset[0], 2)
        x = lax.rem(chip_x + offset[1], across)
        z = lax.rem(chip_z + offset[2], deep)
        return ((z * across + x) * 2 + c, lax.rem(branch + offset[3], BRANCHES))

    along_x = [peer((0, step, 0, 0)) for step in range(1, across)]
    along_z = [peer((0, 0, step, 0)) for step in range(1, deep)]
    along_y = [peer((0, 0, 0, step)) for step in range(1, BRANCHES)]
    partner = peer((1, 0, 0, 0))
    near = [(lax.rem(piece + step, pieces), branch) for step in (1, 2, pieces - 2, pieces - 1)]
    greeted = near + along_z + along_y + along_x + [partner]

    def on(level):
        return pl.when(branch == level)

    def input_copies(level):
        rows, chans, _, _ = sizes(level)
        lanes = max(chans, 128)
        pairs = []
        if level == 0:
            pairs += [(logits, s_logits), (labels, s_labels), (pixel_weight, s_pixel), (head_weight, s_head)]
        pairs += [
            (deriv_outer.at[0, 0, pl.ds(0, rows)], outer.at[pl.ds(0, rows)]),
            (conv_outer.at[0, :, pl.ds(0, chans), pl.ds(0, lanes)], k_outer.at[:, pl.ds(0, chans), pl.ds(0, lanes)]),
            (conv_inner.at[0, :, pl.ds(0, chans), pl.ds(0, lanes)], k_inner.at[:, pl.ds(0, chans), pl.ds(0, lanes)]),
            (deriv_inner.at[0, 0, pl.ds(0, rows)], inner.at[pl.ds(1, rows)]),
        ]
        for other in range(level):
            few = BASE_CH << other
            pairs.append((join_weight.at[level, other, pl.ds(0, chans)], k_join.at[other, pl.ds(0, chans)]))
            pairs.append((join_weight.at[other, level, pl.ds(0, few)], k_join.at[3 + other, pl.ds(0, few)]))
        return [pltpu.make_async_copy(src, dst, in_sem.at[at]) for at, (src, dst) in enumerate(pairs)]

    for level in range(BRANCHES):

        @on(level)
        def _(level=level):
            for copy in input_copies(level):
                copy.start()

    barrier = pltpu.get_barrier_semaphore()
    for other in greeted:
        pl.semaphore_signal(barrier, inc=1, device_id=other, device_id_type=MESH)

    for ref, factor in ((pool2, 2), (pool4, 4), (pool8, 8)):
        row, col = iotas(ref.shape)
        ref[...] = flags(row // factor == col)
    for ref, factor in ((up2, 2), (up4, 4), (up8, 8)):
        row, col = iotas(ref.shape)
        ref[...] = flags(row == col // factor)

    @pl.when(jnp.logical_not(has_above))
    def _():
        inner[0] = jnp.zeros(inner.shape[1:], BF16)
        for turn in range(ITERS):
            for slot in (0, 1):
                scaled[turn, slot] = jnp.zeros(inner.shape[1:], BF16)

    for level in range(BRANCHES):
        rows = sizes(level)[0]

        @pl.when(jnp.logical_and(branch == level, jnp.logical_not(has_below)))
        def _(rows=rows):
            inner[rows + 1] = jnp.zeros(inner.shape[1:], BF16)
            for turn in range(ITERS):
                for slot in (rows + 2, rows + 3):
                    scaled[turn, slot] = jnp.zeros(inner.shape[1:], BF16)

    @pl.when(jnp.logical_and(branch == 3, piece == 1))
    def _():
        for turn in range(ITERS):
            scaled[turn, 0] = jnp.zeros(inner.shape[1:], BF16)

    @pl.when(jnp.logical_and(branch == 3, piece == pieces - 2))
    def _():
        for turn in range(ITERS):
            scaled[turn, 4] = jnp.zeros(inner.shape[1:], BF16)

    def shuffle(level):
        chans, factor = BASE_CH << level, 1 << level
        row, col = iotas((chans, chans))
        return flags(col == factor * lax.rem(row, BASE_CH) + row // BASE_CH)

    def prepare(level):
        rows, chans, _, _ = sizes(level)
        many = GROUP[level]
        order = shuffle(level)
        for which, kernels in enumerate((k_outer, k_inner)):
            for dx in range(3):
                taps = [kernels[3 * dy + dx, :chans, :chans] for dy in (2, 1, 0)]
                if level > 0:
                    taps = [dot(order, tap).astype(BF16) for tap in taps]
                line = dot_nt(order, jnp.concatenate(taps, axis=0)).astype(BF16)
                if many == 1:
                    bands[level][which, dx * chans : (dx + 1) * chans, :] = line
                else:
                    for row_out in range(many):
                        at, to = iotas((3 * chans, (many + 2) * chans))
                        placed = dot(line, flags(to == at + row_out * chans))
                        start = (dx * many + row_out) * chans
                        bands[level][which, start : start + chans, :] = placed.astype(BF16)
        for other in range(level):
            few = BASE_CH << other
            sent = dot(order, k_join[other, :chans, :few]).astype(BF16)
            mix[other, :few, :chans] = dot_nt(shuffle(other), sent).astype(BF16)
            got = dot(shuffle(other), k_join[3 + other, :few, :chans]).astype(BF16)
            mix[3 + other, :chans, :few] = dot_nt(order, got).astype(BF16)

    @on(0)
    def _():
        for copy in input_copies(0)[:5]:
            copy.wait()
        scores = s_logits[...].astype(F32)
        powers = jnp.exp(scores - jnp.max(scores, axis=0, keepdims=True))
        shares = powers / jnp.sum(powers, axis=0, keepdims=True)
        classes = lax.broadcasted_iota(jnp.int32, scores.shape, 0)
        hits = jnp.where(s_labels[...][None] == classes, 1.0, 0.0)
        err = s_pixel[...][None] * (shares - hits)
        count = scores.shape[0]
        flat = err.reshape(count * full_rows, width).astype(BF16)
        row, col = iotas((full_rows * BASE_CH, BASE_CH))
        tall = dot_nt(flags(lax.rem(row, BASE_CH) == col), s_head[...]).astype(BF16)
        row, col = iotas((count, count * full_rows))
        wide = dot(tall, flags(row == col // full_rows))
        row, col = iotas(wide.shape)
        head = jnp.where(row // BASE_CH == lax.rem(col, full_rows), wide, 0.0).astype(BF16)
        first = dot(head, flat)
        for row in range(full_rows):
            own = first[row * BASE_CH : (row + 1) * BASE_CH]
            vecs[0, row] = own
            scaled[0, 2 + row] = (outer[row].astype(F32) * own).astype(BF16)

    @pl.when(branch > 0)
    def _():
        def clear(row, _):
            vecs[0, row] = jnp.zeros(vecs.shape[2:], F32)
            return 0

        lax.fori_loop(0, full_rows, clear, 0)

        def blank(row, _):
            out[row] = jnp.zeros(out.shape[1:], F32)
            return 0

        lax.fori_loop(row_count, full_rows, blank, 0)

    pl.semaphore_wait(barrier, len(greeted))

    circles = (along_x, along_y, [partner])

    def tell(at):
        for other in circles[at]:
            pl.semaphore_signal(known.at[at], inc=1, device_id=other, device_id_type=MESH)

    def hear(at):
        pl.semaphore_wait(known.at[at], len(circles[at]))

    tell(0)

    def rim_copy(level, below):
        rows = sizes(level)[0]
        if below:
            return pltpu.make_async_remote_copy(
                deriv_inner.at[0, 0, rows - 1], inner.at[0], rim_send.at[0], rim_recv.at[0],
                device_id=(piece + 1, branch), device_id_type=MESH,
            )
        return pltpu.make_async_remote_copy(
            deriv_inner.at[0, 0, 0], inner.at[rows + 1], rim_send.at[1], rim_recv.at[1],
            device_id=(piece - 1, branch), device_id_type=MESH,
        )

    def send_rim(level):
        @pl.when(has_below)
        def _():
            rim_copy(level, True).start()

        @pl.when(has_above)
        def _():
            rim_copy(level, False).start()

    def wait_rim(level):
        rows = sizes(level)[0]

        @pl.when(has_above)
        def _():
            wait_all(inner.at[0], rim_recv.at[0])

        @pl.when(has_below)
        def _():
            wait_all(inner.at[rows + 1], rim_recv.at[1])

    def halo_copies(level, turn):
        rows = sizes(level)[0]
        if level < 3:
            plan = [
                (1, slice(rows, rows + 2), slice(0, 2)),
                (-1, slice(2, 4), slice(rows + 2, rows + 4)),
            ]
        else:
            plan = [
                (1, slice(2, 3), slice(1, 2)),
                (-1, slice(2, 3), slice(3, 4)),
                (2, slice(2, 3), slice(0, 1)),
                (-2, slice(2, 3), slice(4, 5)),
            ]
        result = []
        for at, (step, src, dst) in enumerate(plan):
            there = piece + step
            source = piece - step
            copy = pltpu.make_async_remote_copy(
                scaled.at[turn, pl.ds(src.start, src.stop - src.start)],
                scaled.at[turn, pl.ds(dst.start, dst.stop - dst.start)],
                halo_send.at[turn, at],
                halo_recv.at[turn, at],
                device_id=(there, branch),
                device_id_type=MESH,
            )
            sends = there < pieces if step > 0 else there >= 0
            gets = source >= 0 if step > 0 else source < pieces
            result.append((sends, copy, gets))
        return result

    def send_halo(level, turn):
        for sends, copy, _ in halo_copies(level, turn):

            @pl.when(sends)
            def _(copy=copy):
                copy.start()

    def join_copy(level, other, turn):
        pair = (min(level, other), max(level, other))
        return pltpu.make_async_remote_copy(
            gives[pair].at[turn], takes[pair].at[turn], join_send.at[turn, other], join_recv.at[turn, level],
            device_id=(piece, jnp.int32(other)), device_id_type=MESH,
        )

    def chunks(block, level):
        span = width >> level
        return [block[:, at * span : (at + 1) * span] for at in range(1 << level)]

    def grid_rows(load, slots, level):
        return jnp.concatenate([part for slot in slots for part in chunks(load(slot), level)], axis=0)

    def send_terms(level, turn, coarser=None):
        rows, chans, cols, _ = sizes(level)
        load = lambda slot: scaled[turn, slot]
        own = grid_rows(load, range(2, 2 + rows), level)
        for other in coarser or range(level + 1, BRANCHES):
            factor = 1 << (other - level)
            height, less = rows // factor, cols // factor
            ref = gives[(level, other)]
            if factor == 2:
                spans = [(at, pool2[...]) for at in range(cols // 256)]
                pieces_of = [dot(own[:, at * 256 : (at + 1) * 256], mat) for at, mat in spans]
            else:
                mat = pool4[:cols, :less] if factor == 4 else pool8[:cols, :less]
                pieces_of = [dot(own, mat)]
            for at, part in enumerate(pieces_of):
                span = part.shape[1]
                for row in range(height):
                    summed = part[row * factor * chans : (row * factor + 1) * chans]
                    for extra in range(1, factor):
                        start = (row * factor + extra) * chans
                        summed = summed + part[start : start + chans]
                    ref[turn, row * chans : (row + 1) * chans, at * span : (at + 1) * span] = summed.astype(BF16)
            join_copy(level, other, turn).start()
        for other in range(level):
            few = BASE_CH << other
            factor = 1 << (level - other)
            scale = few ** (-0.5) / (factor * factor)
            ref = gives[(other, level)]
            matrix = mix[other, :few, :chans]
            for row in range(rows):
                mixed = dot(matrix, own[row * chans : (row + 1) * chans])
                ref[turn, row * few : (row + 1) * few, :] = (mixed * scale).astype(BF16)
            join_copy(level, other, turn).start()

    def conv(level, which, load, first, many):
        _, chans, _, _ = sizes(level)
        most = GROUP[level]
        band = bands[level]
        right = grid_rows(load, range(first, first + many + 2), level)
        if many == most:
            left = band[which]
        else:
            left = jnp.concatenate(
                [
                    band[which, dx * most * chans : (dx * most + many) * chans, : (many + 2) * chans]
                    for dx in range(3)
                ],
                axis=0,
            )
        prod = dot(left, right)
        size = many * chans
        return prod[size : 2 * size] + shift_cols(prod[2 * size :], 1) + shift_cols(prod[:size], -1)

    def conv_lanes(level, which, load, first, many):
        _, chans, cols, _ = sizes(level)
        right = jnp.concatenate(
            [grid_rows(load, range(first + at, first + at + 3), level) for at in range(many)], axis=1
        )
        prod = dot(bands[level][which], right)
        result = []
        for at in range(many):
            own = prod[:, at * cols : (at + 1) * cols]
            result.append(
                own[chans : 2 * chans] + shift_cols(own[2 * chans :], 1) + shift_cols(own[:chans], -1)
            )
        return result

    def put_w(level, row, values):
        _, chans, cols, factor = sizes(level)
        scale = (9 * chans) ** (-0.5)
        for at in range(factor):
            lanes = slice(at * cols, (at + 1) * cols)
            part = values[at * BASE_CH : (at + 1) * BASE_CH] * scale
            wmap[row + 1, :, lanes] = (inner[row + 1, :, lanes].astype(F32) * part).astype(BF16)

    def put_out(level, turn, to, row, values):
        _, chans, cols, factor = sizes(level)
        scale = (9 * chans) ** (-0.5)
        for at in range(factor):
            lanes = slice(at * cols, (at + 1) * cols)
            part = values[at * BASE_CH : (at + 1) * BASE_CH] * scale
            vecs[to, row, :, lanes] = scaled[turn, 2 + row, :, lanes].astype(F32) + part

    def outer_conv(level, turn, starts):
        chans = BASE_CH << level
        load = lambda slot: scaled[turn, slot]
        for first, many in starts:
            if level == 3:
                for at, values in enumerate(conv_lanes(level, 0, load, first + 1, many)):
                    put_w(level, first + at, values)
            else:
                values = conv(level, 0, load, first + 1, many)
                for at in range(many):
                    put_w(level, first + at, values[at * chans : (at + 1) * chans])

    def inner_conv(level, turn, to, starts):
        chans = BASE_CH << level
        load = lambda slot: wmap[slot]
        for first, many in starts:
            if level == 3:
                for at, values in enumerate(conv_lanes(level, 1, load, first, many)):
                    put_out(level, turn, to, first + at, values)
            else:
                values = conv(level, 1, load, first, many)
                for at in range(many):
                    put_out(level, turn, to, first + at, values[at * chans : (at + 1) * chans])

    inside = ([(1, 6)], [(1, 2)], [], [])
    edges = ([(-1, 2), (7, 2)], [(-1, 2), (3, 2)], [(-1, 1), (0, 1), (1, 1), (2, 1)], [(-1, 3)])
    early = ([(2, 4)], [], [], [])
    finals = ([(0, 2), (6, 2)], [(0, 2), (2, 2)], [(0, 1), (1, 1)], [(0, 1)])
    order = ((0, 1, 6, 7, 2, 3, 4, 5), (0, 1, 2, 3), (0, 1), (0,))
    rims = (4, 4, 2, 1)

    def convs_before(level, turn, to):
        outer_conv(level, turn, inside[level])
        inner_conv(level, turn, to, early[level])

    def convs_after(level, turn, to):
        for _, copy, gets in halo_copies(level, turn):

            @pl.when(gets)
            def _(copy=copy):
                copy.wait_recv()

        outer_conv(level, turn, edges[level])
        inner_conv(level, turn, to, finals[level])

    def term_rows(level, other, turn):
        rows, chans, cols, _ = sizes(level)
        pair = (min(level, other), max(level, other))
        ref = takes[pair]
        wait_all(ref.at[turn], join_recv.at[turn, other])
        if other < level:
            less = BASE_CH << other
            matrix = mix[3 + other, :chans, :less]
            scale = chans ** (-0.5)
            mixed = [dot(matrix, ref[turn, row * less : (row + 1) * less, :]) for row in range(rows)]
            return [(value * scale).astype(BF16).astype(F32) for value in mixed]
        times = 1 << (other - level)
        got = ref[turn]
        if times == 2:
            wide = jnp.concatenate(
                [dot(got[:, at * 128 : (at + 1) * 128], up2[...]) for at in range(cols // 256)], axis=1
            )
        else:
            wide = dot(got, up4[: cols // 4, :cols] if times == 4 else up8[: cols // 8, :cols])
        starts = [(row // times) * chans for row in range(rows)]
        return [wide[start : start + chans] for start in starts]

    def finish(level, turn):
        _, _, cols, factor = sizes(level)
        to = turn + 1
        others = [other for other in range(BRANCHES) if other != level and (turn > 0 or other == 0)]
        terms = [term_rows(level, other, turn) for other in others]
        dots = [jnp.zeros((8, cols), F32)] * ITERS
        for done, row in enumerate(order[level]):
            for at in range(factor):
                lanes = slice(at * cols, (at + 1) * cols)
                parts = [] if level > 0 and turn == 0 else [vecs[to, row, :, lanes]]
                parts += [term[row][at * BASE_CH : (at + 1) * BASE_CH] for term in terms]
                value = parts[0]
                for more in parts[1:]:
                    value = value + more
                vecs[to, row, :, lanes] = value
                if to == ITERS:
                    for left in range(ITERS):
                        prod = vecs[left, row, :, lanes] * value
                        dots[left] = dots[left] + ((prod[0:8] + prod[8:16]) + (prod[16:24] + prod[24:32]))
                else:
                    scaled[to, 2 + row, :, lanes] = (outer[row, :, lanes].astype(F32) * value).astype(BF16)
            if to < ITERS and done + 1 == rims[level]:
                send_halo(level, to)
        if to == ITERS:
            collect(dots, [(left, ITERS) for left in range(ITERS)])

    def products(pairs):
        def step(row, sums):
            result = []
            for have, (left, right) in zip(sums, pairs):
                prod = vecs[left, row] * vecs[right, row]
                result.append(have + ((prod[0:8] + prod[8:16]) + (prod[16:24] + prod[24:32])))
            return tuple(result)

        zero = jnp.zeros((8, width), F32)
        collect(lax.fori_loop(0, row_count, step, (zero,) * len(pairs)), pairs)

    def collect(sums, pairs):
        lane = lax.broadcasted_iota(jnp.int32, part.shape, 1)
        row_of = part[...]
        for value, (left, right) in zip(sums, pairs):
            whole = jnp.sum(jnp.sum(value, axis=0, keepdims=True), axis=1, keepdims=True)
            row_of = row_of + jnp.where(lane == 3 * left + right, whole, 0.0)
        part[...] = row_of

    part[...] = jnp.zeros(part.shape, F32)

    def last_step():
        hear(2)
        mine = piece * BRANCHES + branch
        for there, level in spread:

            @pl.when(jnp.logical_or(piece != there, branch != level))
            def _(there=there, level=level):
                pltpu.make_async_remote_copy(
                    part, took.at[mine], sum_send, sum_recv,
                    device_id=(jnp.int32(there), jnp.int32(level)), device_id_type=MESH,
                ).start()

        wait_all(others, sum_recv)
        took[mine] = part[...]
        sums = jnp.sum(took[...], axis=0)

        def gram(left, right):
            at = 3 * left + right
            return sums[:, at : at + 1]

        g00, g01, g02, g03 = (gram(0, at) for at in range(4))
        g11, g12, g13 = (gram(1, at) for at in range(1, 4))
        g22, g23 = gram(2, 2), gram(2, 3)
        s1 = g00 - g01
        r1 = 1.0 / s1
        k1 = g00 * r1
        rest = 1.0 - k1
        b1, f11 = g01, g11
        b2 = rest * g01 + k1 * g02
        f12 = rest * g11 + k1 * g12
        f2v2 = rest * g12 + k1 * g22
        f22 = rest * f12 + k1 * f2v2
        a1 = b1 - b2
        left1 = k1 * f11 * r1
        s2 = -k1 * (f12 - f11) - left1 * (b2 - b1)
        r2 = 1.0 / s2
        m2 = k1 - 1.0 - a1 * r1
        c22 = -k1 * f12 - left1 * b2
        alpha = 1.0 - c22 * r2
        beta = b2 * r1 - c22 * r2 * m2
        both = k1 + beta
        h1 = (1.0 - both) - alpha * rest
        h2 = both + alpha * rest - alpha * k1
        h3 = alpha * k1
        b3 = h1 * g01 + h2 * g02 + h3 * g03
        f13 = h1 * g11 + h2 * g12 + h3 * g13
        f23 = rest * f13 + k1 * (h1 * g12 + h2 * g22 + h3 * g23)
        a1 = b2 - b3
        a2 = -k1 * (f13 - f12) - left1 * (b3 - b2)
        l1 = (alpha * f12 + beta * f11) * r1
        l2 = (alpha * (f22 + m2 * f12) + beta * (f12 + m2 * f11)) * r2
        s3 = -(alpha * (f23 - f22) + beta * (f13 - f12)) + l1 * a1 + l2 * a2
        r3 = 1.0 / s3
        on2 = alpha - 1.0 - a2 * r2
        on1 = beta - a1 * r1 - a2 * r2 * m2
        c1 = -b3
        c2 = -k1 * f13 - left1 * b3
        c3 = -(alpha * f23 + beta * f13) + l1 * c1 + l2 * c2
        c3 = c3 * r3
        w3 = 1.0 - c3
        w2 = alpha - c2 * r2 - c3 * on2
        w1 = both - c1 * r1 - c2 * r2 * m2 - c3 * on1
        y1 = w1 + w2 * rest + w3 * h1
        y2 = w2 * k1 + w3 * h2
        y3 = w3 * h3

        def fill(row, _):
            out[row] = (vecs[0, row] + y1 * vecs[1, row]) + (y2 * vecs[2, row] + y3 * vecs[3, row])
            return 0

        lax.fori_loop(0, row_count, fill, 0)

    @on(0)
    def _():
        send_halo(0, 0)
        send_terms(0, 0, (3, 2, 1))
        send_rim(0)
        for copy in input_copies(0)[5:]:
            copy.wait()
        prepare(0)

    for level in range(1, BRANCHES):

        @on(level)
        def _(level=level):
            send_rim(level)
            for copy in input_copies(level):
                copy.wait()
            prepare(level)

    def body(turn, _):
        to = turn + 1
        later = turn > 0

        for at in range(2):

            @pl.when(turn == at + 1)
            def _(at=at):
                hear(at)
                tell(at + 1)

        for level in range(BRANCHES):

            @pl.when(jnp.logical_and(branch == level, later))
            def _(level=level):
                send_terms(level, turn)

            @pl.when(jnp.logical_and(branch == level, later if level > 0 else turn >= 0))
            def _(level=level):
                convs_before(level, turn, to)

        @pl.when(turn == 1)
        def _():
            products([(0, 0), (0, 1), (1, 1)])

        @pl.when(turn == 2)
        def _():
            products([(0, 2), (1, 2), (2, 2)])

        for level in range(BRANCHES):

            @pl.when(jnp.logical_and(branch == level, turn == 0))
            def _(level=level):
                wait_rim(level)

            @pl.when(jnp.logical_and(branch == level, later if level > 0 else turn >= 0))
            def _(level=level):
                convs_after(level, turn, to)

            for when in range(ITERS):

                @pl.when(jnp.logical_and(branch == level, turn == when))
                def _(level=level, when=when):
                    finish(level, when)

        return 0

    lax.fori_loop(0, ITERS, body, 0)
    last_step()

    for level in range(BRANCHES):

        @on(level)
        def _(level=level):
            @pl.when(has_below)
            def _():
                rim_copy(level, True).wait_send()

            @pl.when(has_above)
            def _():
                rim_copy(level, False).wait_send()

            for turn in range(0 if level == 0 else 1, ITERS):
                for sends, copy, _ in halo_copies(level, turn):

                    @pl.when(sends)
                    def _(copy=copy):
                        copy.wait_send()

                for other in range(BRANCHES):
                    if other != level:
                        join_copy(level, other, turn).wait_send()

    wait_all(others, sum_send)


def on_device(pieces, *args):
    full_rows, chans, width = args[5].shape[2:]
    across = min(4, pieces // 2)
    classes = args[0].shape[0]
    vmem = pltpu.VMEM

    def band_shape(level):
        size, many = BASE_CH << level, GROUP[level]
        return vmem((2, 3 * many * size, (many + 2) * size), BF16)

    def pair_shape(low, high):
        return vmem((ITERS, full_rows * BASE_CH >> (high - low), width >> high), BF16)

    pairs = [(0, 1), (0, 2), (0, 3), (1, 2), (1, 3), (2, 3)]
    scratch = (
        [
            vmem((classes, full_rows, width), BF16),
            vmem((full_rows, width), jnp.int32),
            vmem((full_rows, width), F32),
            vmem((classes, BASE_CH), BF16),
            vmem((full_rows, chans, width), BF16),
            vmem((full_rows + 2, chans, width), BF16),
            vmem((9, 256, 256), BF16),
            vmem((9, 256, 256), BF16),
            vmem((6, 256, 256), BF16),
        ]
        + [band_shape(level) for level in range(BRANCHES)]
        + [
            vmem((6, 256, 256), BF16),
            vmem((256, 128), BF16),
            vmem((1024, 256), BF16),
            vmem((1024, 128), BF16),
            vmem((128, 256), BF16),
            vmem((256, 1024), BF16),
            vmem((128, 1024), BF16),
            vmem((ITERS, full_rows + 4, chans, width), BF16),
            vmem((full_rows + 2, chans, width), BF16),
            vmem((ITERS + 1, full_rows, chans, width), F32),
        ]
        + [pair_shape(*pair) for pair in pairs] * 2
        + [
            vmem((1, 128), F32),
            vmem((pieces * BRANCHES, 1, 128), F32),
            pltpu.SemaphoreType.REGULAR((3,)),
            pltpu.SemaphoreType.DMA((12,)),
            pltpu.SemaphoreType.DMA((2,)),
            pltpu.SemaphoreType.DMA((2,)),
            pltpu.SemaphoreType.DMA((ITERS, 4)),
            pltpu.SemaphoreType.DMA((ITERS, 4)),
            pltpu.SemaphoreType.DMA((ITERS, 4)),
            pltpu.SemaphoreType.DMA((ITERS, 4)),
            pltpu.SemaphoreType.DMA,
            pltpu.SemaphoreType.DMA,
        ]
    )
    result = pl.pallas_call(
        partial(kernel, pieces, across),
        out_shape=jax.ShapeDtypeStruct((full_rows, chans, width), F32),
        in_specs=[pl.BlockSpec(memory_space=pltpu.HBM)] * 9,
        out_specs=pl.BlockSpec(memory_space=pltpu.VMEM),
        scratch_shapes=scratch,
        compiler_params=pltpu.CompilerParams(
            collective_id=0, has_side_effects=True, vmem_limit_bytes=40 * 1024 * 1024
        ),
    )(*[pltpu.with_memory_space_constraint(arg, pltpu.HBM) for arg in (*args[:3], args[3].T, *args[4:])])
    return result[None, None]


def solution(mesh):
    placed = (
        P(None, "rows", None),
        P("rows", None),
        P("rows", None),
        P(),
        P("branch", "rows", None, None, None),
        P("branch", "rows", None, None, None),
        P("branch", None, None, None),
        P("branch", None, None, None),
        P(),
    )
    return jax.shard_map(
        partial(on_device, mesh.shape["rows"]),
        mesh=mesh,
        in_specs=placed,
        out_specs=P("branch", "rows", None, None, None),
        check_vma=False,
    )
```

```python
from functools import partial

import jax
import jax.numpy as jnp
from jax import lax
from jax.experimental import pallas as pl
from jax.experimental.pallas import tpu as pltpu
from jax.sharding import PartitionSpec as P

BASE_CH = 32
BRANCHES = 4
ITERS = 3
GROUP = (6, 2, 1, 1)
MESH = pl.DeviceIdType.MESH
BF16 = jnp.bfloat16
F32 = jnp.float32


def dot(left, right):
    return jnp.dot(left, right, preferred_element_type=F32)


def dot_nt(left, right):
    return lax.dot_general(left, right, (((1,), (1,)), ((), ())), preferred_element_type=F32)


def iotas(shape):
    return lax.broadcasted_iota(jnp.int32, shape, 0), lax.broadcasted_iota(jnp.int32, shape, 1)


def flags(mask):
    return jnp.where(mask, 1.0, 0.0).astype(BF16)


def shift_cols(values, by):
    width = values.shape[1]
    _, col = iotas(values.shape)
    if by == 1:
        return jnp.where(col == 0, 0.0, pltpu.roll(values, 1, 1))
    return jnp.where(col == width - 1, 0.0, pltpu.roll(values, width - 1, 1))


def wait_all(ref, sem):
    pltpu.make_async_copy(ref, ref, sem).wait()


def kernel(
    pieces,
    across,
    logits,
    labels,
    pixel_weight,
    head_weight,
    deriv_inner,
    deriv_outer,
    conv_inner,
    conv_outer,
    join_weight,
    out,
    s_logits,
    s_labels,
    s_pixel,
    s_head,
    outer,
    inner,
    k_outer,
    k_inner,
    k_join,
    band0,
    band1,
    band2,
    band3,
    mix,
    pool2,
    pool4,
    pool8,
    up2,
    up4,
    up8,
    scaled,
    wmap,
    vecs,
    give01,
    give02,
    give03,
    give12,
    give13,
    give23,
    take01,
    take02,
    take03,
    take12,
    take13,
    take23,
    part,
    took,
    known,
    in_sem,
    rim_send,
    rim_recv,
    halo_send,
    halo_recv,
    join_send,
    join_recv,
    sum_send,
    sum_recv,
):
    piece = lax.axis_index("rows")
    branch = lax.axis_index("branch")
    full_rows, width = outer.shape[0], outer.shape[2]
    row_count = jnp.right_shift(jnp.int32(full_rows), branch)
    bands = (band0, band1, band2, band3)
    gives = {(0, 1): give01, (0, 2): give02, (0, 3): give03, (1, 2): give12, (1, 3): give13, (2, 3): give23}
    takes = {(0, 1): take01, (0, 2): take02, (0, 3): take03, (1, 2): take12, (1, 3): take13, (2, 3): take23}
    has_above = piece > 0
    has_below = piece < pieces - 1
    core, chip_x, chip_z = lax.rem(piece, 2), lax.rem(piece // 2, across), piece // (2 * across)
    deep = pieces // (2 * across)

    def sizes(level):
        return full_rows >> level, BASE_CH << level, width >> level, 1 << level

    spread = [(there, level) for there in range(pieces) for level in range(BRANCHES)]
    spread.sort(key=lambda at: at[0] // (2 * across) + 0.7 * (at[0] // 2 % across) + at[1])
    others = took.at[pl.ds(0, pieces * BRANCHES - 1)]

    def peer(offset):
        c = lax.rem(core + offset[0], 2)
        x = lax.rem(chip_x + offset[1], across)
        z = lax.rem(chip_z + offset[2], deep)
        return ((z * across + x) * 2 + c, lax.rem(branch + offset[3], BRANCHES))

    along_x = [peer((0, step, 0, 0)) for step in range(1, across)]
    along_z = [peer((0, 0, step, 0)) for step in range(1, deep)]
    along_y = [peer((0, 0, 0, step)) for step in range(1, BRANCHES)]
    partner = peer((1, 0, 0, 0))
    near = [(lax.rem(piece + step, pieces), branch) for step in (1, 2, pieces - 2, pieces - 1)]
    greeted = near + along_z + along_y + along_x + [partner]

    def on(level):
        return pl.when(branch == level)

    def input_copies(level):
        rows, chans, _, _ = sizes(level)
        lanes = max(chans, 128)
        pairs = []
        if level == 0:
            pairs += [(logits, s_logits), (labels, s_labels), (pixel_weight, s_pixel), (head_weight, s_head)]
        pairs += [
            (deriv_outer.at[0, 0, pl.ds(0, rows)], outer.at[pl.ds(0, rows)]),
            (conv_outer.at[0, :, pl.ds(0, chans), pl.ds(0, lanes)], k_outer.at[:, pl.ds(0, chans), pl.ds(0, lanes)]),
            (conv_inner.at[0, :, pl.ds(0, chans), pl.ds(0, lanes)], k_inner.at[:, pl.ds(0, chans), pl.ds(0, lanes)]),
            (deriv_inner.at[0, 0, pl.ds(0, rows)], inner.at[pl.ds(1, rows)]),
        ]
        for other in range(level):
            few = BASE_CH << other
            pairs.append((join_weight.at[level, other, pl.ds(0, chans)], k_join.at[other, pl.ds(0, chans)]))
            pairs.append((join_weight.at[other, level, pl.ds(0, few)], k_join.at[3 + other, pl.ds(0, few)]))
        return [pltpu.make_async_copy(src, dst, in_sem.at[at]) for at, (src, dst) in enumerate(pairs)]

    for level in range(BRANCHES):

        @on(level)
        def _(level=level):
            for copy in input_copies(level):
                copy.start()

    barrier = pltpu.get_barrier_semaphore()
    for other in greeted:
        pl.semaphore_signal(barrier, inc=1, device_id=other, device_id_type=MESH)

    for ref, factor in ((pool2, 2), (pool4, 4), (pool8, 8)):
        row, col = iotas(ref.shape)
        ref[...] = flags(row // factor == col)
    for ref, factor in ((up2, 2), (up4, 4), (up8, 8)):
        row, col = iotas(ref.shape)
        ref[...] = flags(row == col // factor)

    @pl.when(jnp.logical_not(has_above))
    def _():
        inner[0] = jnp.zeros(inner.shape[1:], BF16)
        for turn in range(ITERS):
            for slot in (0, 1):
                scaled[turn, slot] = jnp.zeros(inner.shape[1:], BF16)

    for level in range(BRANCHES):
        rows = sizes(level)[0]

        @pl.when(jnp.logical_and(branch == level, jnp.logical_not(has_below)))
        def _(rows=rows):
            inner[rows + 1] = jnp.zeros(inner.shape[1:], BF16)
            for turn in range(ITERS):
                for slot in (rows + 2, rows + 3):
                    scaled[turn, slot] = jnp.zeros(inner.shape[1:], BF16)

    @pl.when(jnp.logical_and(branch == 3, piece == 1))
    def _():
        for turn in range(ITERS):
            scaled[turn, 0] = jnp.zeros(inner.shape[1:], BF16)

    @pl.when(jnp.logical_and(branch == 3, piece == pieces - 2))
    def _():
        for turn in range(ITERS):
            scaled[turn, 4] = jnp.zeros(inner.shape[1:], BF16)

    def shuffle(level):
        chans, factor = BASE_CH << level, 1 << level
        row, col = iotas((chans, chans))
        return flags(col == factor * lax.rem(row, BASE_CH) + row // BASE_CH)

    def prepare(level):
        rows, chans, _, _ = sizes(level)
        many = GROUP[level]
        order = shuffle(level)
        for which, kernels in enumerate((k_outer, k_inner)):
            for dx in range(3):
                taps = [kernels[3 * dy + dx, :chans, :chans] for dy in (2, 1, 0)]
                if level > 0:
                    taps = [dot(order, tap).astype(BF16) for tap in taps]
                line = dot_nt(order, jnp.concatenate(taps, axis=0)).astype(BF16)
                if many == 1:
                    bands[level][which, dx * chans : (dx + 1) * chans, :] = line
                else:
                    for row_out in range(many):
                        at, to = iotas((3 * chans, (many + 2) * chans))
                        placed = dot(line, flags(to == at + row_out * chans))
                        start = (dx * many + row_out) * chans
                        bands[level][which, start : start + chans, :] = placed.astype(BF16)
        for other in range(level):
            few = BASE_CH << other
            sent = dot(order, k_join[other, :chans, :few]).astype(BF16)
            mix[other, :few, :chans] = dot_nt(shuffle(other), sent).astype(BF16)
            got = dot(shuffle(other), k_join[3 + other, :few, :chans]).astype(BF16)
            mix[3 + other, :chans, :few] = dot_nt(order, got).astype(BF16)

    @on(0)
    def _():
        for copy in input_copies(0)[:5]:
            copy.wait()
        scores = s_logits[...].astype(F32)
        powers = jnp.exp(scores - jnp.max(scores, axis=0, keepdims=True))
        shares = powers / jnp.sum(powers, axis=0, keepdims=True)
        classes = lax.broadcasted_iota(jnp.int32, scores.shape, 0)
        hits = jnp.where(s_labels[...][None] == classes, 1.0, 0.0)
        err = s_pixel[...][None] * (shares - hits)
        count = scores.shape[0]
        flat = err.reshape(count * full_rows, width).astype(BF16)
        row, col = iotas((full_rows * BASE_CH, BASE_CH))
        tall = dot_nt(flags(lax.rem(row, BASE_CH) == col), s_head[...]).astype(BF16)
        row, col = iotas((count, count * full_rows))
        wide = dot(tall, flags(row == col // full_rows))
        row, col = iotas(wide.shape)
        head = jnp.where(row // BASE_CH == lax.rem(col, full_rows), wide, 0.0).astype(BF16)
        first = dot(head, flat)
        for row in range(full_rows):
            own = first[row * BASE_CH : (row + 1) * BASE_CH]
            vecs[0, row] = own
            scaled[0, 2 + row] = (outer[row].astype(F32) * own).astype(BF16)

    @pl.when(branch > 0)
    def _():
        def clear(row, _):
            vecs[0, row] = jnp.zeros(vecs.shape[2:], F32)
            return 0

        lax.fori_loop(0, full_rows, clear, 0)

        def blank(row, _):
            out[row] = jnp.zeros(out.shape[1:], F32)
            return 0

        lax.fori_loop(row_count, full_rows, blank, 0)

    pl.semaphore_wait(barrier, len(greeted))

    circles = (along_x, along_y, [partner])

    def tell(at):
        for other in circles[at]:
            pl.semaphore_signal(known.at[at], inc=1, device_id=other, device_id_type=MESH)

    def hear(at):
        pl.semaphore_wait(known.at[at], len(circles[at]))

    tell(0)

    def rim_copy(level, below):
        rows = sizes(level)[0]
        if below:
            return pltpu.make_async_remote_copy(
                deriv_inner.at[0, 0, rows - 1], inner.at[0], rim_send.at[0], rim_recv.at[0],
                device_id=(piece + 1, branch), device_id_type=MESH,
            )
        return pltpu.make_async_remote_copy(
            deriv_inner.at[0, 0, 0], inner.at[rows + 1], rim_send.at[1], rim_recv.at[1],
            device_id=(piece - 1, branch), device_id_type=MESH,
        )

    def send_rim(level):
        @pl.when(has_below)
        def _():
            rim_copy(level, True).start()

        @pl.when(has_above)
        def _():
            rim_copy(level, False).start()

    def wait_rim(level):
        rows = sizes(level)[0]

        @pl.when(has_above)
        def _():
            wait_all(inner.at[0], rim_recv.at[0])

        @pl.when(has_below)
        def _():
            wait_all(inner.at[rows + 1], rim_recv.at[1])

    def halo_copies(level, turn):
        rows = sizes(level)[0]
        if level < 3:
            plan = [
                (1, slice(rows, rows + 2), slice(0, 2)),
                (-1, slice(2, 4), slice(rows + 2, rows + 4)),
            ]
        else:
            plan = [
                (1, slice(2, 3), slice(1, 2)),
                (-1, slice(2, 3), slice(3, 4)),
                (2, slice(2, 3), slice(0, 1)),
                (-2, slice(2, 3), slice(4, 5)),
            ]
        result = []
        for at, (step, src, dst) in enumerate(plan):
            there = piece + step
            source = piece - step
            copy = pltpu.make_async_remote_copy(
                scaled.at[turn, pl.ds(src.start, src.stop - src.start)],
                scaled.at[turn, pl.ds(dst.start, dst.stop - dst.start)],
                halo_send.at[turn, at],
                halo_recv.at[turn, at],
                device_id=(there, branch),
                device_id_type=MESH,
            )
            sends = there < pieces if step > 0 else there >= 0
            gets = source >= 0 if step > 0 else source < pieces
            result.append((sends, copy, gets))
        return result

    def send_halo(level, turn):
        for sends, copy, _ in halo_copies(level, turn):

            @pl.when(sends)
            def _(copy=copy):
                copy.start()

    def join_copy(level, other, turn):
        pair = (min(level, other), max(level, other))
        return pltpu.make_async_remote_copy(
            gives[pair].at[turn], takes[pair].at[turn], join_send.at[turn, other], join_recv.at[turn, level],
            device_id=(piece, jnp.int32(other)), device_id_type=MESH,
        )

    def chunks(block, level):
        span = width >> level
        return [block[:, at * span : (at + 1) * span] for at in range(1 << level)]

    def grid_rows(load, slots, level):
        return jnp.concatenate([part for slot in slots for part in chunks(load(slot), level)], axis=0)

    def send_terms(level, turn, coarser=None):
        rows, chans, cols, _ = sizes(level)
        load = lambda slot: scaled[turn, slot]
        own = grid_rows(load, range(2, 2 + rows), level)
        for other in reversed(range(level)):
            few = BASE_CH << other
            factor = 1 << (level - other)
            scale = few ** (-0.5) / (factor * factor)
            ref = gives[(other, level)]
            matrix = mix[other, :few, :chans]
            for row in range(rows):
                mixed = dot(matrix, own[row * chans : (row + 1) * chans])
                ref[turn, row * few : (row + 1) * few, :] = (mixed * scale).astype(BF16)
            join_copy(level, other, turn).start()
        for other in coarser or range(level + 1, BRANCHES):
            factor = 1 << (other - level)
            height, less = rows // factor, cols // factor
            ref = gives[(level, other)]
            if factor == 2:
                spans = [(at, pool2[...]) for at in range(cols // 256)]
                pieces_of = [dot(own[:, at * 256 : (at + 1) * 256], mat) for at, mat in spans]
            else:
                mat = pool4[:cols, :less] if factor == 4 else pool8[:cols, :less]
                pieces_of = [dot(own, mat)]
            for at, part in enumerate(pieces_of):
                span = part.shape[1]
                for row in range(height):
                    summed = part[row * factor * chans : (row * factor + 1) * chans]
                    for extra in range(1, factor):
                        start = (row * factor + extra) * chans
                        summed = summed + part[start : start + chans]
                    ref[turn, row * chans : (row + 1) * chans, at * span : (at + 1) * span] = summed.astype(BF16)
            join_copy(level, other, turn).start()

    def conv(level, which, load, first, many):
        _, chans, _, _ = sizes(level)
        most = GROUP[level]
        band = bands[level]
        right = grid_rows(load, range(first, first + many + 2), level)
        if many == most:
            left = band[which]
        else:
            left = jnp.concatenate(
                [
                    band[which, dx * most * chans : (dx * most + many) * chans, : (many + 2) * chans]
                    for dx in range(3)
                ],
                axis=0,
            )
        prod = dot(left, right)
        size = many * chans
        return prod[size : 2 * size] + shift_cols(prod[2 * size :], 1) + shift_cols(prod[:size], -1)

    def conv_lanes(level, which, load, first, many):
        _, chans, cols, _ = sizes(level)
        right = jnp.concatenate(
            [grid_rows(load, range(first + at, first + at + 3), level) for at in range(many)], axis=1
        )
        prod = dot(bands[level][which], right)
        result = []
        for at in range(many):
            own = prod[:, at * cols : (at + 1) * cols]
            result.append(
                own[chans : 2 * chans] + shift_cols(own[2 * chans :], 1) + shift_cols(own[:chans], -1)
            )
        return result

    def put_w(level, row, values):
        _, chans, cols, factor = sizes(level)
        scale = (9 * chans) ** (-0.5)
        for at in range(factor):
            lanes = slice(at * cols, (at + 1) * cols)
            part = values[at * BASE_CH : (at + 1) * BASE_CH] * scale
            wmap[row + 1, :, lanes] = (inner[row + 1, :, lanes].astype(F32) * part).astype(BF16)

    def put_out(level, turn, to, row, values):
        _, chans, cols, factor = sizes(level)
        scale = (9 * chans) ** (-0.5)
        for at in range(factor):
            lanes = slice(at * cols, (at + 1) * cols)
            part = values[at * BASE_CH : (at + 1) * BASE_CH] * scale
            vecs[to, row, :, lanes] = scaled[turn, 2 + row, :, lanes].astype(F32) + part

    def outer_conv(level, turn, starts):
        chans = BASE_CH << level
        load = lambda slot: scaled[turn, slot]
        for first, many in starts:
            if level == 3:
                for at, values in enumerate(conv_lanes(level, 0, load, first + 1, many)):
                    put_w(level, first + at, values)
            else:
                values = conv(level, 0, load, first + 1, many)
                for at in range(many):
                    put_w(level, first + at, values[at * chans : (at + 1) * chans])

    def inner_conv(level, turn, to, starts):
        chans = BASE_CH << level
        load = lambda slot: wmap[slot]
        for first, many in starts:
            if level == 3:
                for at, values in enumerate(conv_lanes(level, 1, load, first, many)):
                    put_out(level, turn, to, first + at, values)
            else:
                values = conv(level, 1, load, first, many)
                for at in range(many):
                    put_out(level, turn, to, first + at, values[at * chans : (at + 1) * chans])

    inside = ([(1, 6)], [(1, 2)], [], [])
    edges = ([(-1, 2), (7, 2)], [(-1, 2), (3, 2)], [(-1, 1), (0, 1), (1, 1), (2, 1)], [(-1, 3)])
    early = ([(2, 4)], [], [], [])
    finals = ([(0, 2), (6, 2)], [(0, 2), (2, 2)], [(0, 1), (1, 1)], [(0, 1)])
    order = ((0, 1, 6, 7, 2, 3, 4, 5), (0, 1, 2, 3), (0, 1), (0,))
    rims = (4, 4, 2, 1)

    def convs_before(level, turn, to):
        outer_conv(level, turn, inside[level])
        inner_conv(level, turn, to, early[level])

    def convs_after(level, turn, to):
        for _, copy, gets in halo_copies(level, turn):

            @pl.when(gets)
            def _(copy=copy):
                copy.wait_recv()

        outer_conv(level, turn, edges[level])
        inner_conv(level, turn, to, finals[level])

    def term_rows(level, other, turn):
        rows, chans, cols, _ = sizes(level)
        pair = (min(level, other), max(level, other))
        ref = takes[pair]
        wait_all(ref.at[turn], join_recv.at[turn, other])
        if other < level:
            less = BASE_CH << other
            matrix = mix[3 + other, :chans, :less]
            scale = chans ** (-0.5)
            mixed = [dot(matrix, ref[turn, row * less : (row + 1) * less, :]) for row in range(rows)]
            return [(value * scale).astype(BF16).astype(F32) for value in mixed]
        times = 1 << (other - level)
        got = ref[turn]
        if times == 2:
            wide = jnp.concatenate(
                [dot(got[:, at * 128 : (at + 1) * 128], up2[...]) for at in range(cols // 256)], axis=1
            )
        else:
            wide = dot(got, up4[: cols // 4, :cols] if times == 4 else up8[: cols // 8, :cols])
        starts = [(row // times) * chans for row in range(rows)]
        return [wide[start : start + chans] for start in starts]

    def finish(level, turn):
        _, _, cols, factor = sizes(level)
        to = turn + 1
        others = [other for other in ((3, 2, 1), (3, 2, 0), (3, 0, 1), (0, 1, 2))[level] if turn > 0 or other == 0]
        terms = [term_rows(level, other, turn) for other in others]
        dots = [jnp.zeros((8, cols), F32)] * ITERS
        for done, row in enumerate(order[level]):
            for at in range(factor):
                lanes = slice(at * cols, (at + 1) * cols)
                parts = [] if level > 0 and turn == 0 else [vecs[to, row, :, lanes]]
                parts += [term[row][at * BASE_CH : (at + 1) * BASE_CH] for term in terms]
                value = parts[0]
                for more in parts[1:]:
                    value = value + more
                vecs[to, row, :, lanes] = value
                if to == ITERS:
                    for left in range(ITERS):
                        prod = vecs[left, row, :, lanes] * value
                        dots[left] = dots[left] + ((prod[0:8] + prod[8:16]) + (prod[16:24] + prod[24:32]))
                else:
                    scaled[to, 2 + row, :, lanes] = (outer[row, :, lanes].astype(F32) * value).astype(BF16)
            if to < ITERS and done + 1 == rims[level]:
                send_halo(level, to)
        if to == ITERS:
            collect(dots, [(left, ITERS) for left in range(ITERS)])

    def products(pairs):
        def step(row, sums):
            result = []
            for have, (left, right) in zip(sums, pairs):
                prod = vecs[left, row] * vecs[right, row]
                result.append(have + ((prod[0:8] + prod[8:16]) + (prod[16:24] + prod[24:32])))
            return tuple(result)

        zero = jnp.zeros((8, width), F32)
        collect(lax.fori_loop(0, row_count, step, (zero,) * len(pairs)), pairs)

    def collect(sums, pairs):
        lane = lax.broadcasted_iota(jnp.int32, part.shape, 1)
        row_of = part[...]
        for value, (left, right) in zip(sums, pairs):
            whole = jnp.sum(jnp.sum(value, axis=0, keepdims=True), axis=1, keepdims=True)
            row_of = row_of + jnp.where(lane == 3 * left + right, whole, 0.0)
        part[...] = row_of

    part[...] = jnp.zeros(part.shape, F32)

    def last_step():
        hear(2)
        mine = piece * BRANCHES + branch
        for there, level in spread:

            @pl.when(jnp.logical_or(piece != there, branch != level))
            def _(there=there, level=level):
                pltpu.make_async_remote_copy(
                    part, took.at[mine], sum_send, sum_recv,
                    device_id=(jnp.int32(there), jnp.int32(level)), device_id_type=MESH,
                ).start()

        wait_all(others, sum_recv)
        took[mine] = part[...]
        sums = jnp.sum(took[...], axis=0)

        def gram(left, right):
            at = 3 * left + right
            return sums[:, at : at + 1]

        g00, g01, g02, g03 = (gram(0, at) for at in range(4))
        g11, g12, g13 = (gram(1, at) for at in range(1, 4))
        g22, g23 = gram(2, 2), gram(2, 3)
        s1 = g00 - g01
        r1 = 1.0 / s1
        k1 = g00 * r1
        rest = 1.0 - k1
        b1, f11 = g01, g11
        b2 = rest * g01 + k1 * g02
        f12 = rest * g11 + k1 * g12
        f2v2 = rest * g12 + k1 * g22
        f22 = rest * f12 + k1 * f2v2
        a1 = b1 - b2
        left1 = k1 * f11 * r1
        s2 = -k1 * (f12 - f11) - left1 * (b2 - b1)
        r2 = 1.0 / s2
        m2 = k1 - 1.0 - a1 * r1
        c22 = -k1 * f12 - left1 * b2
        alpha = 1.0 - c22 * r2
        beta = b2 * r1 - c22 * r2 * m2
        both = k1 + beta
        h1 = (1.0 - both) - alpha * rest
        h2 = both + alpha * rest - alpha * k1
        h3 = alpha * k1
        b3 = h1 * g01 + h2 * g02 + h3 * g03
        f13 = h1 * g11 + h2 * g12 + h3 * g13
        f23 = rest * f13 + k1 * (h1 * g12 + h2 * g22 + h3 * g23)
        a1 = b2 - b3
        a2 = -k1 * (f13 - f12) - left1 * (b3 - b2)
        l1 = (alpha * f12 + beta * f11) * r1
        l2 = (alpha * (f22 + m2 * f12) + beta * (f12 + m2 * f11)) * r2
        s3 = -(alpha * (f23 - f22) + beta * (f13 - f12)) + l1 * a1 + l2 * a2
        r3 = 1.0 / s3
        on2 = alpha - 1.0 - a2 * r2
        on1 = beta - a1 * r1 - a2 * r2 * m2
        c1 = -b3
        c2 = -k1 * f13 - left1 * b3
        c3 = -(alpha * f23 + beta * f13) + l1 * c1 + l2 * c2
        c3 = c3 * r3
        w3 = 1.0 - c3
        w2 = alpha - c2 * r2 - c3 * on2
        w1 = both - c1 * r1 - c2 * r2 * m2 - c3 * on1
        y1 = w1 + w2 * rest + w3 * h1
        y2 = w2 * k1 + w3 * h2
        y3 = w3 * h3

        def fill(row, _):
            out[row] = (vecs[0, row] + y1 * vecs[1, row]) + (y2 * vecs[2, row] + y3 * vecs[3, row])
            return 0

        lax.fori_loop(0, row_count, fill, 0)

    @on(0)
    def _():
        send_halo(0, 0)
        send_terms(0, 0, (3, 2, 1))
        send_rim(0)
        for copy in input_copies(0)[5:]:
            copy.wait()
        prepare(0)

    for level in range(1, BRANCHES):

        @on(level)
        def _(level=level):
            send_rim(level)
            for copy in input_copies(level):
                copy.wait()
            prepare(level)

    def body(turn, _):
        to = turn + 1
        later = turn > 0

        for at in range(2):

            @pl.when(turn == at + 1)
            def _(at=at):
                hear(at)
                tell(at + 1)

        for level in range(BRANCHES):

            @pl.when(jnp.logical_and(branch == level, later))
            def _(level=level):
                send_terms(level, turn)

            @pl.when(jnp.logical_and(branch == level, later if level > 0 else turn >= 0))
            def _(level=level):
                convs_before(level, turn, to)

        @pl.when(turn == 1)
        def _():
            products([(0, 0), (0, 1), (1, 1)])

        @pl.when(turn == 2)
        def _():
            products([(0, 2), (1, 2), (2, 2)])

        for level in range(BRANCHES):

            @pl.when(jnp.logical_and(branch == level, turn == 0))
            def _(level=level):
                wait_rim(level)

            @pl.when(jnp.logical_and(branch == level, later if level > 0 else turn >= 0))
            def _(level=level):
                convs_after(level, turn, to)

            for when in range(ITERS):

                @pl.when(jnp.logical_and(branch == level, turn == when))
                def _(level=level, when=when):
                    finish(level, when)

        return 0

    lax.fori_loop(0, ITERS, body, 0)
    last_step()

    for level in range(BRANCHES):

        @on(level)
        def _(level=level):
            @pl.when(has_below)
            def _():
                rim_copy(level, True).wait_send()

            @pl.when(has_above)
            def _():
                rim_copy(level, False).wait_send()

            for turn in range(0 if level == 0 else 1, ITERS):
                for sends, copy, _ in halo_copies(level, turn):

                    @pl.when(sends)
                    def _(copy=copy):
                        copy.wait_send()

                for other in range(BRANCHES):
                    if other != level:
                        join_copy(level, other, turn).wait_send()

    wait_all(others, sum_send)


def on_device(pieces, *args):
    full_rows, chans, width = args[5].shape[2:]
    across = min(4, pieces // 2)
    classes = args[0].shape[0]
    vmem = pltpu.VMEM

    def band_shape(level):
        size, many = BASE_CH << level, GROUP[level]
        return vmem((2, 3 * many * size, (many + 2) * size), BF16)

    def pair_shape(low, high):
        return vmem((ITERS, full_rows * BASE_CH >> (high - low), width >> high), BF16)

    pairs = [(0, 1), (0, 2), (0, 3), (1, 2), (1, 3), (2, 3)]
    scratch = (
        [
            vmem((classes, full_rows, width), BF16),
            vmem((full_rows, width), jnp.int32),
            vmem((full_rows, width), F32),
            vmem((classes, BASE_CH), BF16),
            vmem((full_rows, chans, width), BF16),
            vmem((full_rows + 2, chans, width), BF16),
            vmem((9, 256, 256), BF16),
            vmem((9, 256, 256), BF16),
            vmem((6, 256, 256), BF16),
        ]
        + [band_shape(level) for level in range(BRANCHES)]
        + [
            vmem((6, 256, 256), BF16),
            vmem((256, 128), BF16),
            vmem((1024, 256), BF16),
            vmem((1024, 128), BF16),
            vmem((128, 256), BF16),
            vmem((256, 1024), BF16),
            vmem((128, 1024), BF16),
            vmem((ITERS, full_rows + 4, chans, width), BF16),
            vmem((full_rows + 2, chans, width), BF16),
            vmem((ITERS + 1, full_rows, chans, width), F32),
        ]
        + [pair_shape(*pair) for pair in pairs] * 2
        + [
            vmem((1, 128), F32),
            vmem((pieces * BRANCHES, 1, 128), F32),
            pltpu.SemaphoreType.REGULAR((3,)),
            pltpu.SemaphoreType.DMA((12,)),
            pltpu.SemaphoreType.DMA((2,)),
            pltpu.SemaphoreType.DMA((2,)),
            pltpu.SemaphoreType.DMA((ITERS, 4)),
            pltpu.SemaphoreType.DMA((ITERS, 4)),
            pltpu.SemaphoreType.DMA((ITERS, 4)),
            pltpu.SemaphoreType.DMA((ITERS, 4)),
            pltpu.SemaphoreType.DMA,
            pltpu.SemaphoreType.DMA,
        ]
    )
    result = pl.pallas_call(
        partial(kernel, pieces, across),
        out_shape=jax.ShapeDtypeStruct((full_rows, chans, width), F32),
        in_specs=[pl.BlockSpec(memory_space=pltpu.HBM)] * 9,
        out_specs=pl.BlockSpec(memory_space=pltpu.VMEM),
        scratch_shapes=scratch,
        compiler_params=pltpu.CompilerParams(
            collective_id=0, has_side_effects=True, vmem_limit_bytes=40 * 1024 * 1024
        ),
    )(*[pltpu.with_memory_space_constraint(arg, pltpu.HBM) for arg in (*args[:3], args[3].T, *args[4:])])
    return result[None, None]


def solution(mesh):
    placed = (
        P(None, "rows", None),
        P("rows", None),
        P("rows", None),
        P(),
        P("branch", "rows", None, None, None),
        P("branch", "rows", None, None, None),
        P("branch", None, None, None),
        P("branch", None, None, None),
        P(),
    )
    return jax.shard_map(
        partial(on_device, mesh.shape["rows"]),
        mesh=mesh,
        in_specs=placed,
        out_specs=P("branch", "rows", None, None, None),
        check_vma=False,
    )
```
